32 devices in a mesh: row: 4 (over x, core), col: 8 (over z, y).
Axes of the slice: x: 2, y: 2, z: 4, core: 2. Of those that a mesh axis runs over, the one named last changes fastest.
Arguments:
- amplitudes: float32 [4096, 2048], P('row', 'col'), may hold values from -6 to 6
- pp_integrals: float32 [2048, 2048], P('row', 'col'), may hold values from -2.5 to 2.5
- hole_fock: float32 [64, 64], replicated, may hold values from -0.75 to 0.75
- tile_pattern: int32 [64, 32], P('row', 'col'), may hold values 0 or 1
- integral_pattern: int32 [32, 32], P('row', 'col'), may hold values 0 or 1
- tile_extent: int32 [32], P('col'), may hold values from 40 to 64
- tile_owner: int32 [8, 4], P('col'), may hold values from 0 to 3, each once within a row
Outputs:
- residual_owned: float32 [32, 64, 4096], P(('row', 'col'))
The draws below stay inside these ranges and needn't reach their ends.
Inputs may be any that keep to these rules, and one draw needn't show every extreme that they name: Each row of tile_owner names every tile of its group once.
All inputs are finite; a program needn't handle non-finite values. No bound on the sum of `tile_pattern` or of `integral_pattern` on one device may be relied on, other than what follows from the above.
Results may differ from the reference program's by a relative error of at most 0.000067.
Values sent between devices are 32-bit elements; how exact they have to be, the bound alone decides.
No kernel may reach another device: no remote copies, remote signals or barrier semaphores. Data moves between devices by JAX's collectives and lax.ppermute only.
A program may use at most 128 MiB of HBM per device.

```python
import jax
import jax.numpy as jnp
from jax import lax

NO = 64
TS = 64
VT_DEV = 1
OPAIRS = 4096
VT = 32
VPAIRS = 2048
GROUP_TILES = 4
N_ROW = 4
N_COL = 8


def with_ends(result, stream_key, low, high):
    longest = result.shape.index(max(result.shape))
    spots = []
    for shift in (0, 1):
        where = [jax.random.randint(jax.random.fold_in(stream_key, axis), (), 0, length) for axis, length in enumerate(result.shape)]
        where[longest] = (where[longest] + shift) % result.shape[longest]
        spots.append(tuple(where))
    return result.at[spots[0]].set(low).at[spots[1]].set(high)


def levels(stream_key, extent, split, least, top_value):
    def one(position, blocks):
        draws = jax.random.uniform(jax.random.fold_in(jax.random.fold_in(stream_key, 6), position), (blocks,), jnp.float32, least / len(split), top_value / len(split))
        return jnp.repeat(jnp.exp(draws), extent[position] // blocks).reshape((-1,) + (1,) * (len(extent) - position - 1))

    level = one(*split[0])
    for cut in split[1:]:
        level = level * one(*cut)
    return level


def scatter_about(key, dims, scale, limit, shards=(), kind=jnp.bfloat16):
    entries = scale * jax.random.normal(key, dims, jnp.float32)
    if shards:
        entries = entries * levels(key, dims, shards, -0.22, 0.18)
    return jnp.clip(entries, -limit, limit).astype(kind)


def setup_inputs(seed: int = 0) -> dict:
    key_list = jax.random.split(jax.random.key(seed), 8)
    amplitudes = scatter_about(key_list[0], (OPAIRS, VPAIRS), 1.0, 6.0, ((0, 4), (1, 8)), jnp.float32)
    pp_integrals = scatter_about(key_list[1], (VPAIRS, VPAIRS), (max(VPAIRS // 400, 1)) ** -0.5, 2.5, ((0, 4), (1, 8)), jnp.float32)
    hole_fock = scatter_about(key_list[2], (NO, NO), NO ** -0.5, 0.75, (), jnp.float32)
    tile_pattern = with_ends((jax.random.randint(key_list[3], (OPAIRS // TS, VT), 0, 20) < 1).astype(jnp.int32), jax.random.fold_in(key_list[3], 1), 0, 1)
    integral_pattern = with_ends((jax.random.randint(key_list[4], (VT, VT), 0, 20) < 1).astype(jnp.int32), jax.random.fold_in(key_list[4], 1), 0, 1)
    tile_extent = with_ends(jax.random.randint(key_list[5], (VT,), TS // 2 + TS // 8, TS + 1), jax.random.fold_in(key_list[5], 1), TS // 2 + TS // 8, TS).astype(jnp.int32)
    tile_owner = jax.vmap(lambda own: jax.random.permutation(own, GROUP_TILES))(jax.random.split(key_list[6], N_COL)).reshape((N_COL, GROUP_TILES)).astype(jnp.int32)
    return {"amplitudes": amplitudes, "pp_integrals": pp_integrals, "hole_fock": hole_fock, "tile_pattern": tile_pattern, "integral_pattern": integral_pattern, "tile_extent": tile_extent, "tile_owner": tile_owner}


def tile_mask(pattern, extents):
    positions = jnp.arange(pattern.shape[1] * TS) % TS
    col_keep = (positions < jnp.repeat(extents, TS)).astype(jnp.float32)
    spread = jnp.repeat(jnp.repeat(pattern.astype(jnp.float32), TS, 0), TS, 1)
    return spread * col_keep[None, :]


def reference(amplitudes, pp_integrals, hole_fock, tile_pattern, integral_pattern, tile_extent, tile_owner):
    highest = lax.Precision.HIGHEST
    keep_mask = tile_mask(tile_pattern, tile_extent)
    masked = amplitudes * keep_mask
    integrals = pp_integrals * jnp.repeat(jnp.repeat(integral_pattern.astype(jnp.float32), TS, 0), TS, 1)
    ladder = jnp.dot(masked, integrals, precision=highest, preferred_element_type=jnp.float32)
    paired = masked.reshape(NO, NO, VPAIRS)
    occupied = jnp.einsum("ik,kjc->ijc", hole_fock, paired, precision=highest)
    occupied = occupied + jnp.einsum("jk,ikc->ijc", hole_fock, paired, precision=highest)
    full = (ladder + occupied.reshape(OPAIRS, VPAIRS)) * keep_mask
    row_ids = jnp.arange(N_ROW, dtype=jnp.int32)[:, None, None]
    col_ids = jnp.arange(N_COL, dtype=jnp.int32)[None, :, None]
    slot_ids = jnp.arange(VT_DEV, dtype=jnp.int32)[None, None, :]
    tile_ids = col_ids * GROUP_TILES + tile_owner[col_ids, row_ids * VT_DEV + slot_ids]
    tile_ids = tile_ids.reshape(-1).astype(jnp.int32)
    blocks = full.reshape(OPAIRS, VT, TS)
    chosen = jnp.take(blocks, tile_ids, axis=1)
    return jnp.transpose(chosen, (1, 2, 0))
```

```python
import jax
import jax.numpy as jnp
from jax import lax
from jax.experimental import pallas as pl
from jax.experimental.pallas import tpu as pltpu
from jax.sharding import PartitionSpec as P

NO = 64
TS = 64
HALF = TS // 2
LANES = 2 * TS
ROW_SLOTS = 8
COL_SLOTS = 2
FLAG_ROWS = 8
HIGHEST = lax.Precision.HIGHEST


def gather_exchange(values, axis):
    count = lax.axis_size(axis)
    copies = jnp.broadcast_to(values[None], (count,) + values.shape)
    return lax.all_to_all(copies, axis, split_axis=0, concat_axis=0)


def occupied_term(moved, hole_fock):
    shape_in = moved.shape
    paired = moved.reshape(NO, NO, shape_in[1] * shape_in[2])
    result = jnp.einsum("ik,kjc->ijc", hole_fock, paired, precision=HIGHEST)
    result = result + jnp.einsum("jk,ikc->ijc", hole_fock, paired, precision=HIGHEST)
    return result.reshape(shape_in)


def dense(
    amplitudes, pp_integrals, hole_fock, tile_pattern, integral_pattern, tile_extent, tile_owner
):
    row_count, col_count = amplitudes.shape
    groups = tile_extent.shape[0]
    col_keep = (lax.broadcasted_iota(jnp.int32, (groups, TS), 1) < tile_extent[:, None]).astype(
        jnp.float32
    )
    pattern_float = tile_pattern.astype(jnp.float32)
    keep_mask = (
        jnp.repeat(jnp.repeat(pattern_float, TS, 0), TS, 1) * col_keep.reshape(col_count)[None, :]
    )
    masked = amplitudes * keep_mask
    integrals = pp_integrals * jnp.repeat(
        jnp.repeat(integral_pattern.astype(jnp.float32), TS, 0), TS, 1
    )
    owner_list = tile_owner[0]
    slot_count = groups // lax.axis_size("row")
    my_tiles = lax.dynamic_slice_in_dim(owner_list, lax.axis_index("row") * slot_count, slot_count)

    def ordered(values):
        return jnp.take(values.reshape(values.shape[0], groups, TS), owner_list, axis=1)

    pattern_sent = jnp.take(pattern_float, owner_list, axis=1)
    column_block = gather_exchange(integrals, "row")
    column_block = column_block.reshape(-1, col_count)
    row_block = gather_exchange(masked, "col")
    row_block = jnp.transpose(row_block, (1, 0, 2)).reshape(row_count, -1)
    ladder = jnp.dot(
        row_block, column_block, precision=HIGHEST, preferred_element_type=jnp.float32
    )
    moved_amps, moved_ladder, moved_pattern = (
        lax.all_to_all(ordered(masked), "row", split_axis=1, concat_axis=0, tiled=True),
        lax.all_to_all(ordered(ladder), "row", split_axis=1, concat_axis=0, tiled=True),
        lax.all_to_all(pattern_sent, "row", split_axis=1, concat_axis=0, tiled=True),
    )
    occupied = occupied_term(moved_amps, hole_fock)
    extents = jnp.take(tile_extent, my_tiles)
    extent_keep = (lax.broadcasted_iota(jnp.int32, (slot_count, TS), 1) < extents[:, None]).astype(
        jnp.float32
    )
    final_keep = jnp.repeat(moved_pattern, TS, 0)[:, :, None] * extent_keep[None, :, :]
    full = (moved_ladder + occupied) * final_keep
    return jnp.transpose(full, (1, 2, 0))


class Layout:
    def __init__(self, rows, cols, row_tiles, integral_tiles, groups):
        self.rows, self.cols, self.groups = rows, cols, groups
        self.row_tiles, self.integral_tiles = row_tiles, integral_tiles
        self.integral_at = groups * row_tiles
        self.owner_at = self.integral_at + groups * integral_tiles
        self.width = -(-(self.owner_at + groups) // 128) * 128
        self.row_message = ROW_SLOTS * HALF + FLAG_ROWS
        self.col_message = COL_SLOTS * HALF + FLAG_ROWS

    def amp(self, info, row, tile, col, local):
        return info[row * self.cols + col, 0, local * self.row_tiles + tile]

    def integral(self, info, row, tile, col, local):
        return info[row * self.cols + col, 0, self.integral_at + local * self.integral_tiles + tile]

    def owner(self, info, row, col):
        return info[col, 0, self.owner_at + row]


def load_transposed(source, turn, tile, local, extent):
    lanes = pl.multiple_of((local // 2) * LANES, LANES)
    rows = pl.multiple_of(tile * TS, TS)
    turn[...] = source[pl.ds(rows, TS), pl.ds(lanes, LANES)].T
    start = pl.multiple_of((local % 2) * TS, TS)
    upper = turn[pl.ds(start, HALF), :]
    lower = turn[pl.ds(start + HALF, HALF), :]
    if extent is not None:
        position = lax.broadcasted_iota(jnp.int32, (HALF, TS), 0)
        upper = jnp.where(position < extent, upper, 0.0)
        lower = jnp.where(position + HALF < extent, lower, 0.0)
    return jnp.concatenate([upper, lower], axis=1)


def unfold(packed):
    return jnp.concatenate([packed[:, :TS], packed[:, TS:]], axis=0)


def pack_kernel(lay, info, extent, amps, ints, col_out, row_out, turn, amp_list, int_list, counts):
    row, col = lax.axis_index("row"), lax.axis_index("col")
    overflow = jnp.int32(0)
    n_amp = jnp.int32(0)
    n_int = jnp.int32(0)
    for target in range(lay.rows):
        local = lay.owner(info, target, col)
        used = jnp.int32(0)
        for tile in range(lay.row_tiles):
            hit = lay.amp(info, row, tile, col, local)
            amp_list[n_amp] = ((target * 256 + used) * 256 + tile) * 256 + local
            n_amp += hit
            used += hit
        for tile in range(lay.integral_tiles):
            hit = lay.integral(info, row, tile, col, local)
            int_list[n_int] = ((target * 256 + used) * 256 + tile) * 256 + local
            n_int += hit
            used += hit
        overflow = jnp.maximum(overflow, used)

    def place(source, items, with_extent):
        def body(index, carry):
            item = items[index]
            local, tile, slot, target = item % 256, item // 256 % 256, item // 65536 % 256, item // 16777216

            @pl.when(slot < ROW_SLOTS)
            def _():
                value = load_transposed(
                    source, turn, tile, local, extent[local] if with_extent else None
                )
                row_out[target, pl.ds(pl.multiple_of(slot * HALF, HALF), HALF), :] = value

            return carry

        return body

    lax.fori_loop(0, n_amp, place(amps, amp_list, True), 0)
    lax.fori_loop(0, n_int, place(ints, int_list, False), 0)
    for target in range(lay.cols):
        counts[target] = 0
    int_row = (col * lay.groups) // lay.integral_tiles

    def scan(index, worst):
        item = amp_list[index]
        local, tile = item % 256, item // 256 % 256
        int_tile = (col * lay.groups) % lay.integral_tiles + local
        found = jnp.int32(0)
        for target in range(lay.cols):
            for other in range(lay.groups):
                hit = lay.amp(info, row, tile, target, other) * lay.integral(
                    info, int_row, int_tile, target, other
                )
                int_list[found] = target
                found += hit

        def send(step, worst):
            target = int_list[step]
            slot = counts[target]
            counts[target] = slot + 1

            @pl.when(slot < COL_SLOTS)
            def _():
                value = load_transposed(amps, turn, tile, local, extent[local])
                col_out[target, pl.ds(pl.multiple_of(slot * HALF, HALF), HALF), :] = value

            return jnp.maximum(worst, slot + 1)

        return lax.fori_loop(0, found, send, worst)

    n_scan = jnp.int32(0)
    for tile in range(lay.row_tiles):
        for local in range(lay.groups):
            amp_list[n_scan] = tile * 256 + local
            n_scan += lay.amp(info, row, tile, col, local)
    worst = lax.fori_loop(0, n_scan, scan, jnp.int32(0))
    bad = ((overflow > ROW_SLOTS) | (worst > COL_SLOTS)).astype(jnp.float32)
    flag = jnp.full((lay.cols, FLAG_ROWS, LANES), bad, jnp.float32)
    col_out[:, COL_SLOTS * HALF :, :] = flag


def relay_kernel(lay, info, received, row_in, row_out, tiles, counts, slots, flag, sem):
    del row_in
    row, col = lax.axis_index("row"), lax.axis_index("col")
    for source in range(lay.cols):
        counts[source] = 0
    for target in range(lay.rows):
        local = lay.owner(info, target, col)
        used = jnp.int32(0)
        for tile in range(lay.row_tiles):
            used += lay.amp(info, row, tile, col, local)
        for tile in range(lay.integral_tiles):
            used += lay.integral(info, row, tile, col, local)
        slots[local] = used
        slots[lay.groups + local] = target
    worst = jnp.int32(0)

    def per_tile(tile, worst):
        present = jnp.int32(0)
        for local in range(lay.groups):
            present += lay.amp(info, row, tile, col, local)

        def scan(worst):
            found = jnp.int32(0)
            for source in range(lay.cols):
                for middle in range(lay.groups):
                    tiles[found] = source * lay.groups + middle
                    found += lay.amp(info, row, tile, source, middle)

            def per_middle(index, worst):
                middle = tiles[index]
                source = middle // lay.groups
                int_row, int_tile = middle // lay.integral_tiles, middle % lay.integral_tiles
                for local in range(lay.groups):
                    hit = lay.amp(info, row, tile, col, local) * lay.integral(
                        info, int_row, int_tile, col, local
                    )

                    def move():
                        taken = counts[source]
                        counts[source] = taken + 1
                        slot = slots[local]
                        slots[local] = slot + 1
                        target = slots[lay.groups + local]

                        @pl.when((taken < COL_SLOTS) & (slot < ROW_SLOTS))
                        def _():
                            copy = pltpu.make_async_copy(
                                received.at[
                                    source, pl.ds(pl.multiple_of(taken * HALF, HALF), HALF), :
                                ],
                                row_out.at[
                                    target, pl.ds(pl.multiple_of(slot * HALF, HALF), HALF), :
                                ],
                                sem,
                            )
                            copy.start()
                            copy.wait()

                        return slot + 1

                    worst = jnp.maximum(worst, lax.cond(hit > 0, move, lambda: jnp.int32(0)))
                return worst

            return lax.fori_loop(0, found, per_middle, worst)

        return lax.cond(present > 0, scan, lambda worst: worst, worst)

    worst = lax.fori_loop(0, lay.row_tiles, per_tile, worst)
    seen = jnp.max(received[:, COL_SLOTS * HALF :, :], axis=0)
    seen = jnp.maximum(seen, (worst > ROW_SLOTS).astype(jnp.float32))
    flag[...] = seen
    for target in range(lay.rows):
        copy = pltpu.make_async_copy(
            flag, row_out.at[target, pl.ds(ROW_SLOTS * HALF, FLAG_ROWS), :], sem
        )
        copy.start()
        copy.wait()


def finish_kernel(
    lay, info, extent, fock_scalar, fock, received, out, amp_id, amp_slot, int_id, int_slot, next_slot, total
):
    row, col = lax.axis_index("row"), lax.axis_index("col")
    local = lay.owner(info, row, col)
    limit = extent[local]
    out[...] = jnp.zeros_like(out)
    n_amp = jnp.int32(0)
    n_int = jnp.int32(0)
    for source in range(lay.rows):
        used = jnp.int32(source * lay.row_message)
        for tile in range(lay.row_tiles):
            hit = lay.amp(info, source, tile, col, local)
            amp_id[n_amp] = source * lay.row_tiles + tile
            amp_slot[n_amp] = used
            n_amp += hit
            used += hit * HALF
        for tile in range(lay.integral_tiles):
            hit = lay.integral(info, source, tile, col, local)
            int_id[n_int] = source * lay.integral_tiles + tile
            int_slot[n_int] = used
            n_int += hit
            used += hit * HALF
        next_slot[source] = used

    def load(start):
        return unfold(received[pl.ds(pl.multiple_of(start, 8), HALF), :])

    keep = lax.broadcasted_iota(jnp.int32, (TS, TS), 0) < limit

    def per_tile(index, carry):
        tile = amp_id[index]
        source, within = tile // lay.row_tiles, tile % lay.row_tiles
        total[...] = lax.dot_general(
            load(amp_slot[index]),
            fock[...],
            (((1,), (1,)), ((), ())),
            precision=HIGHEST,
            preferred_element_type=jnp.float32,
        )

        def occupied(other, carry):
            total[...] += fock_scalar[tile, amp_id[other]] * load(amp_slot[other])
            return carry

        lax.fori_loop(0, n_amp, occupied, 0)

        def ladder(other, carry):
            middle = int_id[other]

            @pl.when(
                lay.amp(info, source, within, middle // lay.groups, middle % lay.groups) > 0
            )
            def _():
                start = next_slot[source]
                next_slot[source] = start + HALF
                total[...] += jnp.dot(
                    load(int_slot[other]),
                    load(start),
                    precision=HIGHEST,
                    preferred_element_type=jnp.float32,
                )

            return carry

        lax.fori_loop(0, n_int, ladder, 0)
        value = jnp.where(keep, total[...], 0.0)
        lanes = pl.ds(pl.multiple_of((tile // 2) * LANES, LANES), LANES)
        side = lax.broadcasted_iota(jnp.int32, (TS, LANES), 1) // TS == tile % 2
        out[0, :, lanes] = jnp.where(
            side, jnp.concatenate([value, value], axis=1), out[0, :, lanes]
        )
        return carry

    lax.fori_loop(0, n_amp, per_tile, 0)


def local(
    amplitudes, pp_integrals, hole_fock, tile_pattern, integral_pattern, tile_extent, tile_owner
):
    rows, cols = lax.axis_size("row"), lax.axis_size("col")
    groups = tile_extent.shape[0]
    arguments = (
        amplitudes,
        pp_integrals,
        hole_fock,
        tile_pattern,
        integral_pattern,
        tile_extent,
        tile_owner,
    )
    row_tiles, integral_tiles = tile_pattern.shape[0], integral_pattern.shape[0]
    if groups != rows or integral_tiles % groups:
        return dense(*arguments)
    lay = Layout(rows, cols, row_tiles, integral_tiles, groups)
    devices = rows * cols

    def smem(shape):
        return pltpu.SMEM(shape, jnp.int32)

    in_smem = pl.BlockSpec(memory_space=pltpu.SMEM)
    in_vmem = pl.BlockSpec(memory_space=pltpu.VMEM)
    anywhere = pl.BlockSpec(memory_space=pl.ANY)
    params = pltpu.CompilerParams(vmem_limit_bytes=32 * 2**20)

    mine = jnp.concatenate(
        [
            tile_pattern.T.reshape(-1),
            integral_pattern.T.reshape(-1),
            tile_owner[0],
            jnp.zeros((lay.width - lay.owner_at - groups,), jnp.int32),
        ]
    )
    info = lax.all_to_all(
        jnp.broadcast_to(mine[None, None, :], (devices, 1, lay.width)),
        ("row", "col"),
        split_axis=0,
        concat_axis=0,
        tiled=True,
    )

    col_send, row_part = pl.pallas_call(
        lambda *refs: pack_kernel(lay, *refs),
        out_shape=(
            jax.ShapeDtypeStruct((cols, lay.col_message, LANES), jnp.float32),
            jax.ShapeDtypeStruct((rows, lay.row_message, LANES), jnp.float32),
        ),
        in_specs=[in_smem, in_smem, in_vmem, in_vmem],
        out_specs=(in_vmem, in_vmem),
        scratch_shapes=[
            pltpu.VMEM((LANES, TS), jnp.float32),
            smem((row_tiles * groups + 1,)),
            smem((max(integral_tiles * groups, cols * groups) + 1,)),
            smem((cols,)),
        ],
        compiler_params=params,
        name="pack_tiles",
    )(info, tile_extent, amplitudes, pp_integrals)
    col_received = lax.all_to_all(col_send, "col", split_axis=0, concat_axis=0, tiled=True)
    row_send = pl.pallas_call(
        lambda *refs: relay_kernel(lay, *refs),
        out_shape=jax.ShapeDtypeStruct(row_part.shape, jnp.float32),
        in_specs=[in_smem, in_vmem, anywhere],
        out_specs=anywhere,
        scratch_shapes=[
            smem((cols * groups + 1,)),
            smem((cols,)),
            smem((2 * groups,)),
            pltpu.VMEM((FLAG_ROWS, LANES), jnp.float32),
            pltpu.SemaphoreType.DMA,
        ],
        input_output_aliases={2: 0},
        compiler_params=params,
        name="relay_tiles",
    )(info, col_received, row_part)
    row_received = lax.all_to_all(row_send, "row", split_axis=0, concat_axis=0, tiled=True)
    crowded = jnp.max(row_received[:, ROW_SLOTS * HALF, 0]) > 0

    def finish(info, row_received, *arguments):
        return pl.pallas_call(
            lambda *refs: finish_kernel(lay, *refs),
            out_shape=jax.ShapeDtypeStruct((1, TS, rows * row_tiles * TS), jnp.float32),
            in_specs=[in_smem, in_smem, in_smem, in_vmem, in_vmem],
            out_specs=in_vmem,
            scratch_shapes=[
                smem((rows * row_tiles + 1,)),
                smem((rows * row_tiles + 1,)),
                smem((rows * integral_tiles + 1,)),
                smem((rows * integral_tiles + 1,)),
                smem((rows,)),
                pltpu.VMEM((TS, TS), jnp.float32),
            ],
            compiler_params=params,
            name="finish_residual",
        )(
            info,
            arguments[5],
            arguments[2],
            arguments[2],
            row_received.reshape(rows * lay.row_message, LANES),
        )

    def all_tiles(info, row_received, *arguments):
        return dense(*arguments)

    return lax.cond(crowded, all_tiles, finish, info, row_received, *arguments)


def solution(mesh):
    placed = (
        P("row", "col"),
        P("row", "col"),
        P(),
        P("row", "col"),
        P("row", "col"),
        P("col"),
        P("col", None),
    )
    return jax.shard_map(
        local, mesh=mesh, in_specs=placed, out_specs=P(("row", "col"), None, None), check_vma=False
    )
```

```python
import jax
import jax.numpy as jnp
from jax import lax
from jax.experimental import pallas as pl
from jax.experimental.pallas import tpu as pltpu
from jax.sharding import PartitionSpec as P

NO = 64
TS = 64
HALF = TS // 2
LANES = 2 * TS
ROW_SLOTS = 16
COL_SLOTS = 2
HIGHEST = lax.Precision.HIGHEST


def gather_exchange(values, axis):
    count = lax.axis_size(axis)
    copies = jnp.broadcast_to(values[None], (count,) + values.shape)
    return lax.all_to_all(copies, axis, split_axis=0, concat_axis=0)


def occupied_term(moved, hole_fock):
    shape_in = moved.shape
    paired = moved.reshape(NO, NO, shape_in[1] * shape_in[2])
    result = jnp.einsum("ik,kjc->ijc", hole_fock, paired, precision=HIGHEST)
    result = result + jnp.einsum("jk,ikc->ijc", hole_fock, paired, precision=HIGHEST)
    return result.reshape(shape_in)


def dense(
    amplitudes, pp_integrals, hole_fock, tile_pattern, integral_pattern, tile_extent, tile_owner
):
    row_count, col_count = amplitudes.shape
    groups = tile_extent.shape[0]
    col_keep = (lax.broadcasted_iota(jnp.int32, (groups, TS), 1) < tile_extent[:, None]).astype(
        jnp.float32
    )
    pattern_float = tile_pattern.astype(jnp.float32)
    keep_mask = (
        jnp.repeat(jnp.repeat(pattern_float, TS, 0), TS, 1) * col_keep.reshape(col_count)[None, :]
    )
    masked = amplitudes * keep_mask
    integrals = pp_integrals * jnp.repeat(
        jnp.repeat(integral_pattern.astype(jnp.float32), TS, 0), TS, 1
    )
    owner_list = tile_owner[0]
    slot_count = groups // lax.axis_size("row")
    my_tiles = lax.dynamic_slice_in_dim(owner_list, lax.axis_index("row") * slot_count, slot_count)

    def ordered(values):
        return jnp.take(values.reshape(values.shape[0], groups, TS), owner_list, axis=1)

    pattern_sent = jnp.take(pattern_float, owner_list, axis=1)
    column_block = gather_exchange(integrals, "row")
    column_block = column_block.reshape(-1, col_count)
    row_block = gather_exchange(masked, "col")
    row_block = jnp.transpose(row_block, (1, 0, 2)).reshape(row_count, -1)
    ladder = jnp.dot(
        row_block, column_block, precision=HIGHEST, preferred_element_type=jnp.float32
    )
    moved_amps, moved_ladder, moved_pattern = (
        lax.all_to_all(ordered(masked), "row", split_axis=1, concat_axis=0, tiled=True),
        lax.all_to_all(ordered(ladder), "row", split_axis=1, concat_axis=0, tiled=True),
        lax.all_to_all(pattern_sent, "row", split_axis=1, concat_axis=0, tiled=True),
    )
    occupied = occupied_term(moved_amps, hole_fock)
    extents = jnp.take(tile_extent, my_tiles)
    extent_keep = (lax.broadcasted_iota(jnp.int32, (slot_count, TS), 1) < extents[:, None]).astype(
        jnp.float32
    )
    final_keep = jnp.repeat(moved_pattern, TS, 0)[:, :, None] * extent_keep[None, :, :]
    full = (moved_ladder + occupied) * final_keep
    return jnp.transpose(full, (1, 2, 0))


class Layout:
    def __init__(self, rows, cols, row_tiles, integral_tiles, groups):
        self.rows, self.cols, self.groups = rows, cols, groups
        self.row_tiles, self.integral_tiles = row_tiles, integral_tiles
        self.integral_at = groups * row_tiles
        self.owner_at = self.integral_at + groups * integral_tiles
        self.count_at = self.owner_at + groups
        self.width = -(-(self.count_at + 1) // 128) * 128

    def amp(self, info, row, tile, col, local):
        return info[row * self.cols + col, 0, local * self.row_tiles + tile]

    def integral(self, info, row, tile, col, local):
        return info[row * self.cols + col, 0, self.integral_at + local * self.integral_tiles + tile]

    def owner(self, info, row, col):
        return info[col, 0, self.owner_at + row]


def present(code):
    return jnp.minimum(code, 1)


def slot_rows(slot):
    return pl.ds(pl.multiple_of(slot * HALF, HALF), HALF)


def load_transposed(source, turn, tile, local, extent):
    lanes = pl.multiple_of((local >> 1) * LANES, LANES)
    rows = pl.multiple_of(tile * TS, TS)
    turn[...] = source[pl.ds(rows, TS), pl.ds(lanes, LANES)].T
    start = pl.multiple_of((local & 1) * TS, TS)
    upper = turn[pl.ds(start, HALF), :]
    lower = turn[pl.ds(start + HALF, HALF), :]
    if extent is not None:
        position = lax.broadcasted_iota(jnp.int32, (HALF, TS), 0)
        upper = jnp.where(position < extent, upper, 0.0)
        lower = jnp.where(position + HALF < extent, lower, 0.0)
    return jnp.concatenate([upper, lower], axis=1)


def unfold(packed):
    return jnp.concatenate([packed[:, :TS], packed[:, TS:]], axis=0)


def fold(tile):
    return jnp.concatenate([tile[:HALF], tile[HALF:]], axis=1)


def iota(shape, axis):
    return lax.broadcasted_iota(jnp.int32, shape, axis)


def pack_kernel(
    lay, amp_bits, int_bits, extent, amp_vec, int_vec, owner_vec, amps, ints, packed, info_out, turn, items
):
    pieces = [amp_vec[q : q + 1, :] for q in range(lay.groups)]
    pieces += [int_vec[q : q + 1, :] for q in range(lay.groups)]
    pieces += [owner_vec[...], jnp.zeros((1, lay.width - lay.count_at), jnp.int32)]
    entries = jnp.concatenate(pieces, axis=1).astype(jnp.float32)
    lane = iota((1, lay.width), 1)
    bits = jnp.where(lane < lay.owner_at, entries, 0.0)
    ahead = (iota((lay.width, lay.width), 0) <= iota((lay.width, lay.width), 1)).astype(jnp.float32)
    ranks = jnp.dot(
        jnp.broadcast_to(bits, (8, lay.width)), ahead, preferred_element_type=jnp.float32
    )[:1]
    row = jnp.where(lane < lay.owner_at, bits * ranks, entries)
    row = jnp.where(lane == lay.count_at, ranks, row).astype(jnp.int32)
    info_out[...] = jnp.broadcast_to(row[None], info_out.shape)
    n_amp = jnp.int32(0)
    for local in range(lay.groups):
        for tile in range(lay.row_tiles):
            items[n_amp] = tile * 256 + local
            n_amp += amp_bits[local, tile]
    n_all = n_amp
    for local in range(lay.groups):
        for tile in range(lay.integral_tiles):
            items[n_all] = tile * 256 + local
            n_all += int_bits[local, tile]

    def place(source, with_extent):
        def body(slot, carry):
            item = items[slot]
            local, tile = item & 255, item >> 8
            packed[slot_rows(slot), :] = load_transposed(
                source, turn, tile, local, extent[local] if with_extent else None
            )
            return carry

        return body

    n_amp = jnp.minimum(n_amp, ROW_SLOTS)
    n_all = jnp.minimum(n_all, ROW_SLOTS)
    lax.fori_loop(0, n_amp, place(amps, True), 0)
    lax.fori_loop(n_amp, n_all, place(ints, False), 0)


def check_kernel(lay, info, result):
    codes = info[:, 0, :]
    here = jnp.minimum(codes, 1).astype(jnp.float32)
    lane = iota((1, lay.width), 1)
    contract = (((1,), (1,)), ((), ()))

    def field(start, length, block):
        shift = (lay.width - start) % lay.width
        moved = pltpu.roll(here, shift, 1) if shift else here
        return jnp.where(lane < length, moved, 0.0).reshape(lay.rows, lay.cols, lay.width)[block]

    shared = None
    for row in range(lay.rows):
        stack = jnp.concatenate(
            [field(q * lay.row_tiles, lay.row_tiles, row) for q in range(lay.groups)], axis=0
        )
        term = lax.dot_general(stack, stack, contract, preferred_element_type=jnp.float32)
        shared = term if shared is None else shared + term
    total = lay.groups * lay.cols
    tiles = lay.rows * lay.integral_tiles
    at, to = iota((total, tiles), 0), iota((total, tiles), 1)
    order = (at == (to % lay.groups) * lay.cols + to // lay.groups).astype(jnp.float32)
    shared = jnp.dot(shared, order, preferred_element_type=jnp.float32)
    counts = None
    for row in range(lay.rows):
        stack = jnp.concatenate(
            [
                field(lay.integral_at + q * lay.integral_tiles, lay.integral_tiles, row)
                for q in range(lay.groups)
            ],
            axis=0,
        )
        wide = stack[:, : lay.integral_tiles]
        mine = wide * shared[:, row * lay.integral_tiles : (row + 1) * lay.integral_tiles]
        at, to = iota((lay.integral_tiles, 128), 0), iota((lay.integral_tiles, 128), 1)
        group = (at // lay.groups == to).astype(jnp.float32)
        term = jnp.dot(mine, group, preferred_element_type=jnp.float32)
        counts = term if counts is None else jnp.maximum(counts, term)
    crowded = jnp.max(counts) > COL_SLOTS
    used = jnp.max(jnp.where(lane == lay.count_at, codes, 0))
    result[0] = (crowded | (used > ROW_SLOTS)).astype(jnp.int32)


def forward_kernel(lay, info, *refs):
    packed, (out, pairs, lists) = refs[: lay.rows], refs[lay.rows :]
    row, col = lax.axis_index("row"), lax.axis_index("col")
    base = col * lay.groups
    int_row, int_tile = base // lay.integral_tiles, base % lay.integral_tiles
    n_pairs = jnp.int32(0)
    for target in range(lay.cols):
        wanted = lay.owner(info, row, target)
        for local in range(lay.groups):
            pairs[n_pairs] = target * 256 + local
            n_pairs += present(lay.integral(info, int_row, int_tile + local, target, wanted))

    def scan(index, carry):
        counts, previous, slot = carry
        pair = pairs[index]
        local, target = pair & 255, pair >> 8
        wanted = lay.owner(info, row, target)
        slot = jnp.where(target == previous, slot, 0)
        updated = []
        for k in range(lay.rows):
            count = counts[k]
            for tile in range(lay.row_tiles):
                code = lay.amp(info, row ^ k, tile, col, local)
                hit = present(code * lay.amp(info, row ^ k, tile, target, wanted))
                lists[k, count] = ((target * 256) + jnp.minimum(slot, 255)) * 256 + code - 1
                count += hit
                slot += hit
            updated.append(jnp.minimum(count, lay.cols * COL_SLOTS))
        return tuple(updated), target, slot

    zero = jnp.int32(0)
    counts, _, _ = lax.fori_loop(0, n_pairs, scan, ((zero,) * lay.rows, jnp.int32(-1), zero))
    for k in range(lay.rows):

        def send(index, carry, k=k):
            item = lists[k, index]
            source, slot, target = item & 255, (item >> 8) & 255, item >> 16

            @pl.when((slot < COL_SLOTS) & (source < ROW_SLOTS))
            def _():
                out[target, slot_rows(slot), :] = packed[k][slot_rows(source), :]

            return carry

        lax.fori_loop(0, counts[k], send, 0)


def finish_kernel(lay, info, extent, fock_scalar, fock, received, *refs):
    packed = refs[: lay.rows]
    out, amp_id, int_id, next_slot, tiles, ints, sums = refs[lay.rows :]
    row, col = lax.axis_index("row"), lax.axis_index("col")
    local = lay.owner(info, row, col)
    limit = extent[local]
    out[...] = jnp.zeros_like(out)
    for source in range(lay.cols):
        next_slot[source] = 0
    n_amp = jnp.int32(0)
    n_int = jnp.int32(0)
    for k in range(lay.rows):
        first = n_amp
        for tile in range(lay.row_tiles):
            code = lay.amp(info, row ^ k, tile, col, local)
            amp_id[n_amp] = ((row ^ k) * lay.row_tiles + tile) * 256 + code - 1
            n_amp += present(code)

        def take_amp(index, carry, k=k):
            tiles[slot_rows(index), :] = packed[k][slot_rows(amp_id[index] & 255), :]
            return carry

        lax.fori_loop(first, n_amp, take_amp, 0)
        first = n_int
        for tile in range(lay.integral_tiles):
            code = lay.integral(info, row ^ k, tile, col, local)
            int_id[n_int] = ((row ^ k) * lay.integral_tiles + tile) * 256 + code - 1
            n_int += present(code)

        def take_int(index, carry, k=k):
            ints[slot_rows(index), :] = packed[k][slot_rows(int_id[index] & 255), :]
            return carry

        lax.fori_loop(first, n_int, take_int, 0)

    blank = jnp.zeros((TS, TS), jnp.float32)
    both = jnp.concatenate(
        [
            jnp.concatenate([fock[...], blank], axis=1),
            jnp.concatenate([blank, fock[...]], axis=1),
        ],
        axis=0,
    )
    chunk = 4 * HALF

    def second(index, carry):
        rows = pl.ds(pl.multiple_of(index * chunk, chunk), chunk)
        sums[rows, :] = lax.dot_general(
            tiles[rows, :],
            both,
            (((1,), (1,)), ((), ())),
            precision=HIGHEST,
            preferred_element_type=jnp.float32,
        )
        return carry

    lax.fori_loop(0, (n_amp + 3) >> 2, second, 0)

    def ladder(which, carry):
        middle = int_id[which] >> 8
        source, middle_local = middle // lay.groups, middle % lay.groups

        def per_tile(index, carry):
            tile = amp_id[index] >> 8
            code = lay.amp(info, tile // lay.row_tiles, tile % lay.row_tiles, source, middle_local)

            @pl.when(code > 0)
            def _():
                slot = next_slot[source]
                next_slot[source] = slot + 1
                product = jnp.dot(
                    unfold(ints[slot_rows(which), :]),
                    unfold(received[source, slot_rows(slot), :]),
                    precision=HIGHEST,
                    preferred_element_type=jnp.float32,
                )
                product = jnp.where(iota((TS, TS), 0) < limit, product, 0.0)
                sums[slot_rows(index), :] += fold(product)

            return carry

        return lax.fori_loop(0, n_amp, per_tile, carry)

    lax.fori_loop(0, n_int, ladder, 0)

    def write(index, carry):
        tile = amp_id[index] >> 8

        def first(other, value):
            return value + fock_scalar[tile, amp_id[other] >> 8] * tiles[slot_rows(other), :]

        value = lax.fori_loop(0, n_amp, first, sums[slot_rows(index), :])
        turned = pltpu.roll(value, TS, 1)
        odd = tile & 1
        lanes = pl.ds(pl.multiple_of((tile >> 1) * LANES, LANES), LANES)
        side = iota((HALF, LANES), 1) // TS == odd
        is_odd = iota((HALF, LANES), 0) * 0 + odd == 1
        upper = jnp.where(is_odd, turned, value)
        lower = jnp.where(is_odd, value, turned)
        out[0, :HALF, lanes] = jnp.where(side, upper, out[0, :HALF, lanes])
        out[0, HALF:, lanes] = jnp.where(side, lower, out[0, HALF:, lanes])
        return carry

    lax.fori_loop(0, n_amp, write, 0)


def local(
    amplitudes, pp_integrals, hole_fock, tile_pattern, integral_pattern, tile_extent, tile_owner
):
    rows, cols = lax.axis_size("row"), lax.axis_size("col")
    groups = tile_extent.shape[0]
    arguments = (
        amplitudes,
        pp_integrals,
        hole_fock,
        tile_pattern,
        integral_pattern,
        tile_extent,
        tile_owner,
    )
    row_tiles, integral_tiles = tile_pattern.shape[0], integral_pattern.shape[0]
    if groups != rows or integral_tiles % groups or rows & (rows - 1):
        return dense(*arguments)
    lay = Layout(rows, cols, row_tiles, integral_tiles, groups)
    devices = rows * cols

    def smem(shape):
        return pltpu.SMEM(shape, jnp.int32)

    in_smem = pl.BlockSpec(memory_space=pltpu.SMEM)
    in_vmem = pl.BlockSpec(memory_space=pltpu.VMEM)
    params = pltpu.CompilerParams(vmem_limit_bytes=32 * 2**20)
    packed_shape = (ROW_SLOTS * HALF, LANES)

    packed, mine = pl.pallas_call(
        lambda *refs: pack_kernel(lay, *refs),
        out_shape=(
            jax.ShapeDtypeStruct(packed_shape, jnp.float32),
            jax.ShapeDtypeStruct((devices, 1, lay.width), jnp.int32),
        ),
        in_specs=[in_smem] * 3 + [in_vmem] * 5,
        out_specs=(in_vmem, in_vmem),
        scratch_shapes=[
            pltpu.VMEM((LANES, TS), jnp.float32),
            smem(((row_tiles + integral_tiles) * groups + 1,)),
        ],
        compiler_params=params,
        name="pack_tiles",
    )(
        tile_pattern.T,
        integral_pattern.T,
        tile_extent,
        tile_pattern.T,
        integral_pattern.T,
        tile_owner,
        amplitudes,
        pp_integrals,
    )
    shares = [packed]
    for k in range(1, rows):
        shares.append(lax.ppermute(packed, "row", [(i, i ^ k) for i in range(rows)]))
    info = lax.all_to_all(mine, ("row", "col"), split_axis=0, concat_axis=0, tiled=True)

    crowded = pl.pallas_call(
        lambda *refs: check_kernel(lay, *refs),
        out_shape=jax.ShapeDtypeStruct((1,), jnp.int32),
        in_specs=[in_vmem],
        out_specs=in_smem,
        compiler_params=params,
        name="check_slots",
    )(info)
    col_send = pl.pallas_call(
        lambda *refs: forward_kernel(lay, *refs),
        out_shape=jax.ShapeDtypeStruct((cols, COL_SLOTS * HALF, LANES), jnp.float32),
        in_specs=[in_smem] + [in_vmem] * rows,
        out_specs=in_vmem,
        scratch_shapes=[
            smem((cols * groups + 1,)),
            smem((rows, cols * COL_SLOTS + row_tiles + 1)),
        ],
        compiler_params=params,
        name="forward_tiles",
    )(info, *shares)
    received = lax.all_to_all(col_send, "col", split_axis=0, concat_axis=0, tiled=True)

    def finish(info, received, *arguments):
        count = len(arguments) - 7
        shares, arguments = arguments[:count], arguments[count:]
        return pl.pallas_call(
            lambda *refs: finish_kernel(lay, *refs),
            out_shape=jax.ShapeDtypeStruct((1, TS, rows * row_tiles * TS), jnp.float32),
            in_specs=[in_smem] * 3 + [in_vmem] * (2 + rows),
            out_specs=in_vmem,
            scratch_shapes=[
                smem((rows * row_tiles + 1,)),
                smem((rows * integral_tiles + 1,)),
                smem((cols,)),
                pltpu.VMEM((rows * (row_tiles + 1) * HALF, LANES), jnp.float32),
                pltpu.VMEM((rows * integral_tiles * HALF, LANES), jnp.float32),
                pltpu.VMEM((rows * (row_tiles + 1) * HALF, LANES), jnp.float32),
            ],
            compiler_params=params,
            name="finish_residual",
        )(info, arguments[5], arguments[2], arguments[2], received, *shares)

    def all_tiles(info, received, *arguments):
        return dense(*arguments[-7:])

    return lax.cond(crowded[0] > 0, all_tiles, finish, info, received, *shares, *arguments)


def solution(mesh):
    placed = (
        P("row", "col"),
        P("row", "col"),
        P(),
        P("row", "col"),
        P("row", "col"),
        P("col"),
        P("col", None),
    )
    return jax.shard_map(
        local, mesh=mesh, in_specs=placed, out_specs=P(("row", "col"), None, None), check_vma=False
    )
```

```python
import jax
import jax.numpy as jnp
from jax import lax
from jax.experimental import pallas as pl
from jax.experimental.pallas import tpu as pltpu
from jax.sharding import PartitionSpec as P

NO = 64
TS = 64
HALF = TS // 2
LANES = 2 * TS
ROW_SLOTS = 16
COL_SLOTS = (2, 4)
HIGHEST = lax.Precision.HIGHEST


def gather_exchange(values, axis):
    count = lax.axis_size(axis)
    copies = jnp.broadcast_to(values[None], (count,) + values.shape)
    return lax.all_to_all(copies, axis, split_axis=0, concat_axis=0)


def occupied_term(moved, hole_fock):
    shape_in = moved.shape
    paired = moved.reshape(NO, NO, shape_in[1] * shape_in[2])
    result = jnp.einsum("ik,kjc->ijc", hole_fock, paired, precision=HIGHEST)
    result = result + jnp.einsum("jk,ikc->ijc", hole_fock, paired, precision=HIGHEST)
    return result.reshape(shape_in)


def dense(
    amplitudes, pp_integrals, hole_fock, tile_pattern, integral_pattern, tile_extent, tile_owner
):
    row_count, col_count = amplitudes.shape
    groups = tile_extent.shape[0]
    col_keep = (lax.broadcasted_iota(jnp.int32, (groups, TS), 1) < tile_extent[:, None]).astype(
        jnp.float32
    )
    pattern_float = tile_pattern.astype(jnp.float32)
    keep_mask = (
        jnp.repeat(jnp.repeat(pattern_float, TS, 0), TS, 1) * col_keep.reshape(col_count)[None, :]
    )
    masked = amplitudes * keep_mask
    integrals = pp_integrals * jnp.repeat(
        jnp.repeat(integral_pattern.astype(jnp.float32), TS, 0), TS, 1
    )
    owner_list = tile_owner[0]
    slot_count = groups // lax.axis_size("row")
    my_tiles = lax.dynamic_slice_in_dim(owner_list, lax.axis_index("row") * slot_count, slot_count)

    def ordered(values):
        return jnp.take(values.reshape(values.shape[0], groups, TS), owner_list, axis=1)

    pattern_sent = jnp.take(pattern_float, owner_list, axis=1)
    column_block = gather_exchange(integrals, "row")
    column_block = column_block.reshape(-1, col_count)
    row_block = gather_exchange(masked, "col")
    row_block = jnp.transpose(row_block, (1, 0, 2)).reshape(row_count, -1)
    ladder = jnp.dot(
        row_block, column_block, precision=HIGHEST, preferred_element_type=jnp.float32
    )
    moved_amps, moved_ladder, moved_pattern = (
        lax.all_to_all(ordered(masked), "row", split_axis=1, concat_axis=0, tiled=True),
        lax.all_to_all(ordered(ladder), "row", split_axis=1, concat_axis=0, tiled=True),
        lax.all_to_all(pattern_sent, "row", split_axis=1, concat_axis=0, tiled=True),
    )
    occupied = occupied_term(moved_amps, hole_fock)
    extents = jnp.take(tile_extent, my_tiles)
    extent_keep = (lax.broadcasted_iota(jnp.int32, (slot_count, TS), 1) < extents[:, None]).astype(
        jnp.float32
    )
    final_keep = jnp.repeat(moved_pattern, TS, 0)[:, :, None] * extent_keep[None, :, :]
    full = (moved_ladder + occupied) * final_keep
    return jnp.transpose(full, (1, 2, 0))


class Layout:
    def __init__(self, rows, cols, row_tiles, integral_tiles, groups):
        self.rows, self.cols, self.groups = rows, cols, groups
        self.row_tiles, self.integral_tiles = row_tiles, integral_tiles
        self.integral_at = groups * row_tiles
        self.owner_at = self.integral_at + groups * integral_tiles
        self.count_at = self.owner_at + groups
        self.width = -(-(self.count_at + 1) // 128) * 128

    def amp(self, info, row, tile, col, local):
        return info[row * self.cols + col, 0, local * self.row_tiles + tile]

    def integral(self, info, row, tile, col, local):
        return info[row * self.cols + col, 0, self.integral_at + local * self.integral_tiles + tile]

    def owner(self, info, row, col):
        return info[col, 0, self.owner_at + row]


def present(code):
    return jnp.minimum(code, 1)


def slot_rows(slot):
    return pl.ds(pl.multiple_of(slot * HALF, HALF), HALF)


def load_transposed(source, turn, tile, local, extent):
    lanes = pl.multiple_of((local >> 1) * LANES, LANES)
    rows = pl.multiple_of(tile * TS, TS)
    turn[...] = source[pl.ds(rows, TS), pl.ds(lanes, LANES)].T
    start = pl.multiple_of((local & 1) * TS, TS)
    upper = turn[pl.ds(start, HALF), :]
    lower = turn[pl.ds(start + HALF, HALF), :]
    if extent is not None:
        position = lax.broadcasted_iota(jnp.int32, (HALF, TS), 0)
        upper = jnp.where(position < extent, upper, 0.0)
        lower = jnp.where(position + HALF < extent, lower, 0.0)
    return jnp.concatenate([upper, lower], axis=1)


def unfold(packed):
    return jnp.concatenate([packed[:, :TS], packed[:, TS:]], axis=0)


def fold(tile):
    return jnp.concatenate([tile[:HALF], tile[HALF:]], axis=1)


def iota(shape, axis):
    return lax.broadcasted_iota(jnp.int32, shape, axis)


def pack_kernel(
    lay, amp_bits, int_bits, extent, amp_vec, int_vec, owner_vec, amps, ints, packed, info_out, turn, items
):
    pieces = [amp_vec[q : q + 1, :] for q in range(lay.groups)]
    pieces += [int_vec[q : q + 1, :] for q in range(lay.groups)]
    pieces += [owner_vec[...], jnp.zeros((1, lay.width - lay.count_at), jnp.int32)]
    entries = jnp.concatenate(pieces, axis=1).astype(jnp.float32)
    lane = iota((1, lay.width), 1)
    bits = jnp.where(lane < lay.owner_at, entries, 0.0)
    ahead = (iota((lay.width, lay.width), 0) <= iota((lay.width, lay.width), 1)).astype(jnp.float32)
    ranks = jnp.dot(
        jnp.broadcast_to(bits, (8, lay.width)), ahead, preferred_element_type=jnp.float32
    )[:1]
    row = jnp.where(lane < lay.owner_at, bits * ranks, entries)
    row = jnp.where(lane == lay.count_at, ranks, row).astype(jnp.int32)
    info_out[...] = jnp.broadcast_to(row[None], info_out.shape)
    n_amp = jnp.int32(0)
    for local in range(lay.groups):
        for tile in range(lay.row_tiles):
            items[n_amp] = tile * 256 + local
            n_amp += amp_bits[local, tile]
    n_all = n_amp
    for local in range(lay.groups):
        for tile in range(lay.integral_tiles):
            items[n_all] = tile * 256 + local
            n_all += int_bits[local, tile]

    def place(source, with_extent):
        def body(slot, carry):
            item = items[slot]
            local, tile = item & 255, item >> 8
            packed[slot_rows(slot), :] = load_transposed(
                source, turn, tile, local, extent[local] if with_extent else None
            )
            return carry

        return body

    n_amp = jnp.minimum(n_amp, ROW_SLOTS)
    n_all = jnp.minimum(n_all, ROW_SLOTS)
    lax.fori_loop(0, n_amp, place(amps, True), 0)
    lax.fori_loop(n_amp, n_all, place(ints, False), 0)


def check_kernel(lay, info, result):
    codes = info[:, 0, :]
    here = jnp.minimum(codes, 1).astype(jnp.float32)
    lane = iota((1, lay.width), 1)
    contract = (((1,), (1,)), ((), ()))

    def field(start, length, block):
        shift = (lay.width - start) % lay.width
        moved = pltpu.roll(here, shift, 1) if shift else here
        return jnp.where(lane < length, moved, 0.0).reshape(lay.rows, lay.cols, lay.width)[block]

    shared = None
    for row in range(lay.rows):
        stack = jnp.concatenate(
            [field(q * lay.row_tiles, lay.row_tiles, row) for q in range(lay.groups)], axis=0
        )
        term = lax.dot_general(stack, stack, contract, preferred_element_type=jnp.float32)
        shared = term if shared is None else shared + term
    total = lay.groups * lay.cols
    tiles = lay.rows * lay.integral_tiles
    at, to = iota((total, tiles), 0), iota((total, tiles), 1)
    order = (at == (to % lay.groups) * lay.cols + to // lay.groups).astype(jnp.float32)
    shared = jnp.dot(shared, order, preferred_element_type=jnp.float32)
    at, to = iota((total, tiles), 0), iota((total, tiles), 1)
    own = to == (at % lay.cols) * lay.groups + at // lay.cols
    shared = jnp.where(own, 0.0, shared)
    counts = None
    for row in range(lay.rows):
        stack = jnp.concatenate(
            [
                field(lay.integral_at + q * lay.integral_tiles, lay.integral_tiles, row)
                for q in range(lay.groups)
            ],
            axis=0,
        )
        wide = stack[:, : lay.integral_tiles]
        mine = wide * shared[:, row * lay.integral_tiles : (row + 1) * lay.integral_tiles]
        at, to = iota((lay.integral_tiles, 128), 0), iota((lay.integral_tiles, 128), 1)
        group = (at // lay.groups == to).astype(jnp.float32)
        term = jnp.dot(mine, group, preferred_element_type=jnp.float32)
        counts = term if counts is None else jnp.maximum(counts, term)
    most = jnp.max(counts)
    used = jnp.max(jnp.where(lane == lay.count_at, codes, 0))
    level = jnp.where(most > COL_SLOTS[0], 1, 0)
    result[0] = jnp.where((most > COL_SLOTS[1]) | (used > ROW_SLOTS), 2, level)


def forward_kernel(lay, slots, info, *refs):
    packed, (out, pairs, lists) = refs[: lay.rows], refs[lay.rows :]
    row, col = lax.axis_index("row"), lax.axis_index("col")
    base = col * lay.groups
    int_row, int_tile = base // lay.integral_tiles, base % lay.integral_tiles
    n_pairs = jnp.int32(0)
    for target in range(lay.cols):
        wanted = lay.owner(info, row, target)
        for local in range(lay.groups):
            pairs[n_pairs] = target * 256 + local
            hit = present(lay.integral(info, int_row, int_tile + local, target, wanted))
            n_pairs += jnp.where((target == col) & (wanted == local), 0, hit)

    def scan(index, carry):
        counts, previous, slot = carry
        pair = pairs[index]
        local, target = pair & 255, pair >> 8
        wanted = lay.owner(info, row, target)
        slot = jnp.where(target == previous, slot, 0)
        updated = []
        for k in range(lay.rows):
            count = counts[k]
            for tile in range(lay.row_tiles):
                code = lay.amp(info, row ^ k, tile, col, local)
                hit = present(code * lay.amp(info, row ^ k, tile, target, wanted))
                lists[k, count] = ((target * 256) + jnp.minimum(slot, 255)) * 256 + code - 1
                count += hit
                slot += hit
            updated.append(jnp.minimum(count, lay.cols * slots))
        return tuple(updated), target, slot

    zero = jnp.int32(0)
    counts, _, _ = lax.fori_loop(0, n_pairs, scan, ((zero,) * lay.rows, jnp.int32(-1), zero))
    for k in range(lay.rows):

        def send(index, carry, k=k):
            item = lists[k, index]
            source, slot, target = item & 255, (item >> 8) & 255, item >> 16

            @pl.when((slot < slots) & (source < ROW_SLOTS))
            def _():
                out[target, slot_rows(slot), :] = packed[k][slot_rows(source), :]

            return carry

        lax.fori_loop(0, counts[k], send, 0)


def finish_kernel(lay, info, extent, fock_scalar, fock, received, *refs):
    packed = refs[: lay.rows]
    out, amp_id, int_id, next_slot, tiles, ints, sums = refs[lay.rows :]
    row, col = lax.axis_index("row"), lax.axis_index("col")
    local = lay.owner(info, row, col)
    limit = extent[local]
    out[...] = jnp.zeros_like(out)
    for source in range(lay.cols):
        next_slot[source] = 0
    n_amp = jnp.int32(0)
    n_int = jnp.int32(0)
    for k in range(lay.rows):
        first = n_amp
        for tile in range(lay.row_tiles):
            code = lay.amp(info, row ^ k, tile, col, local)
            amp_id[n_amp] = ((row ^ k) * lay.row_tiles + tile) * 256 + code - 1
            n_amp += present(code)

        def take_amp(index, carry, k=k):
            tiles[slot_rows(index), :] = packed[k][slot_rows(amp_id[index] & 255), :]
            return carry

        lax.fori_loop(first, n_amp, take_amp, 0)
        first = n_int
        for tile in range(lay.integral_tiles):
            code = lay.integral(info, row ^ k, tile, col, local)
            int_id[n_int] = ((row ^ k) * lay.integral_tiles + tile) * 256 + code - 1
            n_int += present(code)

        def take_int(index, carry, k=k):
            ints[slot_rows(index), :] = packed[k][slot_rows(int_id[index] & 255), :]
            return carry

        lax.fori_loop(first, n_int, take_int, 0)

    blank = jnp.zeros((TS, TS), jnp.float32)
    both = jnp.concatenate(
        [
            jnp.concatenate([fock[...], blank], axis=1),
            jnp.concatenate([blank, fock[...]], axis=1),
        ],
        axis=0,
    )
    chunk = 4 * HALF

    def second(index, carry):
        rows = pl.ds(pl.multiple_of(index * chunk, chunk), chunk)
        sums[rows, :] = lax.dot_general(
            tiles[rows, :],
            both,
            (((1,), (1,)), ((), ())),
            precision=HIGHEST,
            preferred_element_type=jnp.float32,
        )
        return carry

    lax.fori_loop(0, (n_amp + 3) >> 2, second, 0)

    def ladder(which, carry):
        middle = int_id[which] >> 8
        source, middle_local = middle // lay.groups, middle % lay.groups
        own = (source == col) & (middle_local == local)

        def add(index, packed_tile):
            product = jnp.dot(
                unfold(ints[slot_rows(which), :]),
                unfold(packed_tile),
                precision=HIGHEST,
                preferred_element_type=jnp.float32,
            )
            product = jnp.where(iota((TS, TS), 0) < limit, product, 0.0)
            sums[slot_rows(index), :] += fold(product)

        def per_tile(index, carry):
            tile = amp_id[index] >> 8
            code = lay.amp(info, tile // lay.row_tiles, tile % lay.row_tiles, source, middle_local)

            @pl.when(own)
            def _():
                add(index, tiles[slot_rows(index), :])

            @pl.when((code > 0) & ~own)
            def _():
                slot = next_slot[source]
                next_slot[source] = slot + 1
                add(index, received[source, slot_rows(slot), :])

            return carry

        return lax.fori_loop(0, n_amp, per_tile, carry)

    lax.fori_loop(0, n_int, ladder, 0)

    def write(index, carry):
        tile = amp_id[index] >> 8

        def first(other, value):
            return value + fock_scalar[tile, amp_id[other] >> 8] * tiles[slot_rows(other), :]

        value = lax.fori_loop(0, n_amp, first, sums[slot_rows(index), :])
        turned = pltpu.roll(value, TS, 1)
        odd = tile & 1
        lanes = pl.ds(pl.multiple_of((tile >> 1) * LANES, LANES), LANES)
        side = iota((HALF, LANES), 1) // TS == odd
        is_odd = iota((HALF, LANES), 0) * 0 + odd == 1
        upper = jnp.where(is_odd, turned, value)
        lower = jnp.where(is_odd, value, turned)
        out[0, :HALF, lanes] = jnp.where(side, upper, out[0, :HALF, lanes])
        out[0, HALF:, lanes] = jnp.where(side, lower, out[0, HALF:, lanes])
        return carry

    lax.fori_loop(0, n_amp, write, 0)


def local(
    amplitudes, pp_integrals, hole_fock, tile_pattern, integral_pattern, tile_extent, tile_owner
):
    rows, cols = lax.axis_size("row"), lax.axis_size("col")
    groups = tile_extent.shape[0]
    arguments = (
        amplitudes,
        pp_integrals,
        hole_fock,
        tile_pattern,
        integral_pattern,
        tile_extent,
        tile_owner,
    )
    row_tiles, integral_tiles = tile_pattern.shape[0], integral_pattern.shape[0]
    if groups != rows or integral_tiles % groups or rows & (rows - 1):
        return dense(*arguments)
    lay = Layout(rows, cols, row_tiles, integral_tiles, groups)
    devices = rows * cols

    def smem(shape):
        return pltpu.SMEM(shape, jnp.int32)

    in_smem = pl.BlockSpec(memory_space=pltpu.SMEM)
    in_vmem = pl.BlockSpec(memory_space=pltpu.VMEM)
    params = pltpu.CompilerParams(vmem_limit_bytes=32 * 2**20)
    packed_shape = (ROW_SLOTS * HALF, LANES)

    packed, mine = pl.pallas_call(
        lambda *refs: pack_kernel(lay, *refs),
        out_shape=(
            jax.ShapeDtypeStruct(packed_shape, jnp.float32),
            jax.ShapeDtypeStruct((devices, 1, lay.width), jnp.int32),
        ),
        in_specs=[in_smem] * 3 + [in_vmem] * 5,
        out_specs=(in_vmem, in_vmem),
        scratch_shapes=[
            pltpu.VMEM((LANES, TS), jnp.float32),
            smem(((row_tiles + integral_tiles) * groups + 1,)),
        ],
        compiler_params=params,
        name="pack_tiles",
    )(
        tile_pattern.T,
        integral_pattern.T,
        tile_extent,
        tile_pattern.T,
        integral_pattern.T,
        tile_owner,
        amplitudes,
        pp_integrals,
    )
    shares = [packed]
    for k in range(1, rows):
        shares.append(lax.ppermute(packed, "row", [(i, i ^ k) for i in range(rows)]))
    info = lax.all_to_all(mine, ("row", "col"), split_axis=0, concat_axis=0, tiled=True)

    level = pl.pallas_call(
        lambda *refs: check_kernel(lay, *refs),
        out_shape=jax.ShapeDtypeStruct((1,), jnp.int32),
        in_specs=[in_vmem],
        out_specs=in_smem,
        compiler_params=params,
        name="check_slots",
    )(info)

    def forward(slots, info, *shares):
        col_send = pl.pallas_call(
            lambda *refs: forward_kernel(lay, slots, *refs),
            out_shape=jax.ShapeDtypeStruct((cols, slots * HALF, LANES), jnp.float32),
            in_specs=[in_smem] + [in_vmem] * rows,
            out_specs=in_vmem,
            scratch_shapes=[
                smem((cols * groups + 1,)),
                smem((rows, cols * slots + row_tiles + 1)),
            ],
            compiler_params=params,
            name="forward_tiles",
        )(info, *shares)
        return lax.all_to_all(col_send, "col", split_axis=0, concat_axis=0, tiled=True)

    received = forward(COL_SLOTS[0], info, *shares)

    def finish(info, received, shares, arguments):
        return pl.pallas_call(
            lambda *refs: finish_kernel(lay, *refs),
            out_shape=jax.ShapeDtypeStruct((1, TS, rows * row_tiles * TS), jnp.float32),
            in_specs=[in_smem] * 3 + [in_vmem] * (2 + rows),
            out_specs=in_vmem,
            scratch_shapes=[
                smem((rows * row_tiles + 1,)),
                smem((rows * integral_tiles + 1,)),
                smem((cols,)),
                pltpu.VMEM((rows * (row_tiles + 1) * HALF, LANES), jnp.float32),
                pltpu.VMEM((rows * integral_tiles * HALF, LANES), jnp.float32),
                pltpu.VMEM((rows * (row_tiles + 1) * HALF, LANES), jnp.float32),
            ],
            compiler_params=params,
            name="finish_residual",
        )(info, arguments[5], arguments[2], arguments[2], received, *shares)

    def more_slots(info, received, shares, arguments):
        return finish(info, forward(COL_SLOTS[1], info, *shares), shares, arguments)

    def all_tiles(info, received, shares, arguments):
        return dense(*arguments)

    return lax.switch(
        level[0], (finish, more_slots, all_tiles), info, received, tuple(shares), arguments
    )


def solution(mesh):
    placed = (
        P("row", "col"),
        P("row", "col"),
        P(),
        P("row", "col"),
        P("row", "col"),
        P("col"),
        P("col", None),
    )
    return jax.shard_map(
        local, mesh=mesh, in_specs=placed, out_specs=P(("row", "col"), None, None), check_vma=False
    )
```

```python
import jax
import jax.numpy as jnp
from jax import lax
from jax.experimental import pallas as pl
from jax.experimental.pallas import tpu as pltpu
from jax.sharding import PartitionSpec as P

NO = 64
TS = 64
HALF = TS // 2
LANES = 2 * TS
ROW_SLOTS = 16
COL_SLOTS = (2, 4)
HIGHEST = lax.Precision.HIGHEST


def gather_exchange(values, axis):
    count = lax.axis_size(axis)
    copies = jnp.broadcast_to(values[None], (count,) + values.shape)
    return lax.all_to_all(copies, axis, split_axis=0, concat_axis=0)


def occupied_term(moved, hole_fock):
    shape_in = moved.shape
    paired = moved.reshape(NO, NO, shape_in[1] * shape_in[2])
    result = jnp.einsum("ik,kjc->ijc", hole_fock, paired, precision=HIGHEST)
    result = result + jnp.einsum("jk,ikc->ijc", hole_fock, paired, precision=HIGHEST)
    return result.reshape(shape_in)


def dense(
    amplitudes, pp_integrals, hole_fock, tile_pattern, integral_pattern, tile_extent, tile_owner
):
    row_count, col_count = amplitudes.shape
    groups = tile_extent.shape[0]
    col_keep = (lax.broadcasted_iota(jnp.int32, (groups, TS), 1) < tile_extent[:, None]).astype(
        jnp.float32
    )
    pattern_float = tile_pattern.astype(jnp.float32)
    keep_mask = (
        jnp.repeat(jnp.repeat(pattern_float, TS, 0), TS, 1) * col_keep.reshape(col_count)[None, :]
    )
    masked = amplitudes * keep_mask
    integrals = pp_integrals * jnp.repeat(
        jnp.repeat(integral_pattern.astype(jnp.float32), TS, 0), TS, 1
    )
    owner_list = tile_owner[0]
    slot_count = groups // lax.axis_size("row")
    my_tiles = lax.dynamic_slice_in_dim(owner_list, lax.axis_index("row") * slot_count, slot_count)

    def ordered(values):
        return jnp.take(values.reshape(values.shape[0], groups, TS), owner_list, axis=1)

    pattern_sent = jnp.take(pattern_float, owner_list, axis=1)
    column_block = gather_exchange(integrals, "row")
    column_block = column_block.reshape(-1, col_count)
    row_block = gather_exchange(masked, "col")
    row_block = jnp.transpose(row_block, (1, 0, 2)).reshape(row_count, -1)
    ladder = jnp.dot(
        row_block, column_block, precision=HIGHEST, preferred_element_type=jnp.float32
    )
    moved_amps, moved_ladder, moved_pattern = (
        lax.all_to_all(ordered(masked), "row", split_axis=1, concat_axis=0, tiled=True),
        lax.all_to_all(ordered(ladder), "row", split_axis=1, concat_axis=0, tiled=True),
        lax.all_to_all(pattern_sent, "row", split_axis=1, concat_axis=0, tiled=True),
    )
    occupied = occupied_term(moved_amps, hole_fock)
    extents = jnp.take(tile_extent, my_tiles)
    extent_keep = (lax.broadcasted_iota(jnp.int32, (slot_count, TS), 1) < extents[:, None]).astype(
        jnp.float32
    )
    final_keep = jnp.repeat(moved_pattern, TS, 0)[:, :, None] * extent_keep[None, :, :]
    full = (moved_ladder + occupied) * final_keep
    return jnp.transpose(full, (1, 2, 0))


class Layout:
    def __init__(self, rows, cols, row_tiles, integral_tiles, groups):
        self.rows, self.cols, self.groups = rows, cols, groups
        self.row_tiles, self.integral_tiles = row_tiles, integral_tiles
        self.integral_at = groups * row_tiles
        self.owner_at = self.integral_at + groups * integral_tiles
        self.count_at = self.owner_at + groups
        self.width = -(-(self.count_at + 1) // 128) * 128

    def amp(self, info, row, tile, col, local):
        return info[row * self.cols + col, 0, local * self.row_tiles + tile]

    def integral(self, info, row, tile, col, local):
        return info[row * self.cols + col, 0, self.integral_at + local * self.integral_tiles + tile]

    def owner(self, info, row, col):
        return info[col, 0, self.owner_at + row]


def present(code):
    return jnp.minimum(code, 1)


def slot_rows(slot):
    return pl.ds(pl.multiple_of(slot * HALF, HALF), HALF)


def load_transposed(source, turn, tile, local, extent):
    lanes = pl.multiple_of((local >> 1) * LANES, LANES)
    rows = pl.multiple_of(tile * TS, TS)
    turn[...] = source[pl.ds(rows, TS), pl.ds(lanes, LANES)].T
    start = pl.multiple_of((local & 1) * TS, TS)
    upper = turn[pl.ds(start, HALF), :]
    lower = turn[pl.ds(start + HALF, HALF), :]
    if extent is not None:
        position = lax.broadcasted_iota(jnp.int32, (HALF, TS), 0)
        upper = jnp.where(position < extent, upper, 0.0)
        lower = jnp.where(position + HALF < extent, lower, 0.0)
    return jnp.concatenate([upper, lower], axis=1)


def unfold(packed):
    return jnp.concatenate([packed[:, :TS], packed[:, TS:]], axis=0)


def fold(tile):
    return jnp.concatenate([tile[:HALF], tile[HALF:]], axis=1)


def iota(shape, axis):
    return lax.broadcasted_iota(jnp.int32, shape, axis)


def pack_kernel(
    lay, amp_bits, int_bits, extent, amp_vec, int_vec, owner_vec, amps, ints, packed, info_out, turn, items
):
    pieces = [amp_vec[q : q + 1, :] for q in range(lay.groups)]
    pieces += [int_vec[q : q + 1, :] for q in range(lay.groups)]
    pieces += [owner_vec[...], jnp.zeros((1, lay.width - lay.count_at), jnp.int32)]
    entries = jnp.concatenate(pieces, axis=1).astype(jnp.float32)
    lane = iota((1, lay.width), 1)
    bits = jnp.where(lane < lay.owner_at, entries, 0.0)
    ahead = (iota((lay.width, lay.width), 0) <= iota((lay.width, lay.width), 1)).astype(jnp.float32)
    ranks = jnp.dot(
        jnp.broadcast_to(bits, (8, lay.width)), ahead, preferred_element_type=jnp.float32
    )[:1]
    row = jnp.where(lane < lay.owner_at, bits * ranks, entries)
    row = jnp.where(lane == lay.count_at, ranks, row).astype(jnp.int32)
    info_out[...] = jnp.broadcast_to(row[None], info_out.shape)
    n_amp = jnp.int32(0)
    for local in range(lay.groups):
        for tile in range(lay.row_tiles):
            items[n_amp] = tile * 256 + local
            n_amp += amp_bits[local, tile]
    n_all = n_amp
    for local in range(lay.groups):
        for tile in range(lay.integral_tiles):
            items[n_all] = tile * 256 + local
            n_all += int_bits[local, tile]

    def place(source, with_extent):
        def body(slot, carry):
            item = items[slot]
            local, tile = item & 255, item >> 8
            packed[slot_rows(slot), :] = load_transposed(
                source, turn, tile, local, extent[local] if with_extent else None
            )
            return carry

        return body

    n_amp = jnp.minimum(n_amp, ROW_SLOTS)
    n_all = jnp.minimum(n_all, ROW_SLOTS)
    lax.fori_loop(0, n_amp, place(amps, True), 0)
    lax.fori_loop(n_amp, n_all, place(ints, False), 0)


def check_kernel(lay, info, result):
    codes = info[:, 0, :]
    here = jnp.minimum(codes, 1).astype(jnp.float32)
    lane = iota((1, lay.width), 1)
    contract = (((1,), (1,)), ((), ()))

    def field(start, length, block):
        shift = (lay.width - start) % lay.width
        moved = pltpu.roll(here, shift, 1) if shift else here
        return jnp.where(lane < length, moved, 0.0).reshape(lay.rows, lay.cols, lay.width)[block]

    shared = None
    for row in range(lay.rows):
        stack = jnp.concatenate(
            [field(q * lay.row_tiles, lay.row_tiles, row) for q in range(lay.groups)], axis=0
        )
        term = lax.dot_general(stack, stack, contract, preferred_element_type=jnp.float32)
        shared = term if shared is None else shared + term
    total = lay.groups * lay.cols
    tiles = lay.rows * lay.integral_tiles
    at, to = iota((total, tiles), 0), iota((total, tiles), 1)
    order = (at == (to % lay.groups) * lay.cols + to // lay.groups).astype(jnp.float32)
    shared = jnp.dot(shared, order, preferred_element_type=jnp.float32)
    at, to = iota((total, tiles), 0), iota((total, tiles), 1)
    own = to == (at % lay.cols) * lay.groups + at // lay.cols
    shared = jnp.where(own, 0.0, shared)
    counts = None
    for row in range(lay.rows):
        stack = jnp.concatenate(
            [
                field(lay.integral_at + q * lay.integral_tiles, lay.integral_tiles, row)
                for q in range(lay.groups)
            ],
            axis=0,
        )
        wide = stack[:, : lay.integral_tiles]
        mine = wide * shared[:, row * lay.integral_tiles : (row + 1) * lay.integral_tiles]
        at, to = iota((lay.integral_tiles, 128), 0), iota((lay.integral_tiles, 128), 1)
        group = (at // lay.groups == to).astype(jnp.float32)
        term = jnp.dot(mine, group, preferred_element_type=jnp.float32)
        counts = term if counts is None else jnp.maximum(counts, term)
    most = jnp.max(counts)
    used = jnp.max(jnp.where(lane == lay.count_at, codes, 0))
    level = jnp.where(most > COL_SLOTS[0], 1, 0)
    result[0] = jnp.where((most > COL_SLOTS[1]) | (used > ROW_SLOTS), 2, level)


def forward_kernel(lay, slots, info, *refs):
    packed, outs = refs[: lay.rows], refs[lay.rows : lay.rows + lay.cols]
    out, pairs, lists = refs[lay.rows + lay.cols :]
    row, col = lax.axis_index("row"), lax.axis_index("col")
    base = col * lay.groups
    int_row, int_tile = base // lay.integral_tiles, base % lay.integral_tiles
    n_pairs = jnp.int32(0)
    for target in range(lay.cols):
        wanted = lay.owner(info, row, target)
        for local in range(lay.groups):
            pairs[n_pairs] = target * 256 + local
            hit = present(lay.integral(info, int_row, int_tile + local, target, wanted))
            n_pairs += jnp.where((target == col) & (wanted == local), 0, hit)

    def scan(index, carry):
        counts, previous, slot = carry
        pair = pairs[index]
        local, target = pair & 255, pair >> 8
        wanted = lay.owner(info, row, target)
        slot = jnp.where(target == previous, slot, 0)
        updated = []
        for k in range(lay.rows):
            count = counts[k]
            for tile in range(lay.row_tiles):
                code = lay.amp(info, row ^ k, tile, col, local)
                hit = present(code * lay.amp(info, row ^ k, tile, target, wanted))
                lists[k, count] = ((target * 256) + jnp.minimum(slot, 255)) * 256 + code - 1
                count += hit
                slot += hit
            updated.append(jnp.minimum(count, lay.cols * slots))
        return tuple(updated), target, slot

    zero = jnp.int32(0)
    counts, _, _ = lax.fori_loop(0, n_pairs, scan, ((zero,) * lay.rows, jnp.int32(-1), zero))
    for k in range(lay.rows):

        def send(index, carry, k=k):
            item = lists[k, index]
            source, slot, target = item & 255, (item >> 8) & 255, item >> 16

            @pl.when((slot < slots) & (source < ROW_SLOTS))
            def _():
                out[target ^ col, slot_rows(slot), :] = packed[k][slot_rows(source), :]

            return carry

        lax.fori_loop(0, counts[k], send, 0)
    for k in range(lay.cols):
        outs[k][...] = out[k]


def finish_kernel(lay, info, extent, fock_scalar, fock, *refs):
    packed, messages = refs[: lay.rows], refs[lay.rows : lay.rows + lay.cols]
    out, amp_id, int_id, next_slot, tiles, ints, sums, received = refs[lay.rows + lay.cols :]
    row, col = lax.axis_index("row"), lax.axis_index("col")
    local = lay.owner(info, row, col)
    limit = extent[local]
    out[...] = jnp.zeros_like(out)
    for source in range(lay.cols):
        next_slot[source] = 0
        received[source] = messages[source][...]
    n_amp = jnp.int32(0)
    n_int = jnp.int32(0)
    for k in range(lay.rows):
        first = n_amp
        for tile in range(lay.row_tiles):
            code = lay.amp(info, row ^ k, tile, col, local)
            amp_id[n_amp] = ((row ^ k) * lay.row_tiles + tile) * 256 + code - 1
            n_amp += present(code)

        def take_amp(index, carry, k=k):
            tiles[slot_rows(index), :] = packed[k][slot_rows(amp_id[index] & 255), :]
            return carry

        lax.fori_loop(first, n_amp, take_amp, 0)
        first = n_int
        for tile in range(lay.integral_tiles):
            code = lay.integral(info, row ^ k, tile, col, local)
            int_id[n_int] = ((row ^ k) * lay.integral_tiles + tile) * 256 + code - 1
            n_int += present(code)

        def take_int(index, carry, k=k):
            ints[slot_rows(index), :] = packed[k][slot_rows(int_id[index] & 255), :]
            return carry

        lax.fori_loop(first, n_int, take_int, 0)

    blank = jnp.zeros((TS, TS), jnp.float32)
    both = jnp.concatenate(
        [
            jnp.concatenate([fock[...], blank], axis=1),
            jnp.concatenate([blank, fock[...]], axis=1),
        ],
        axis=0,
    )
    chunk = 4 * HALF

    def second(index, carry):
        rows = pl.ds(pl.multiple_of(index * chunk, chunk), chunk)
        sums[rows, :] = lax.dot_general(
            tiles[rows, :],
            both,
            (((1,), (1,)), ((), ())),
            precision=HIGHEST,
            preferred_element_type=jnp.float32,
        )
        return carry

    lax.fori_loop(0, (n_amp + 3) >> 2, second, 0)

    def ladder(which, carry):
        middle = int_id[which] >> 8
        source, middle_local = middle // lay.groups, middle % lay.groups
        own = (source == col) & (middle_local == local)

        def add(index, packed_tile):
            product = jnp.dot(
                unfold(ints[slot_rows(which), :]),
                unfold(packed_tile),
                precision=HIGHEST,
                preferred_element_type=jnp.float32,
            )
            product = jnp.where(iota((TS, TS), 0) < limit, product, 0.0)
            sums[slot_rows(index), :] += fold(product)

        def per_tile(index, carry):
            tile = amp_id[index] >> 8
            code = lay.amp(info, tile // lay.row_tiles, tile % lay.row_tiles, source, middle_local)

            @pl.when(own)
            def _():
                add(index, tiles[slot_rows(index), :])

            @pl.when((code > 0) & ~own)
            def _():
                slot = next_slot[source]
                next_slot[source] = slot + 1
                add(index, received[source ^ col, slot_rows(slot), :])

            return carry

        return lax.fori_loop(0, n_amp, per_tile, carry)

    lax.fori_loop(0, n_int, ladder, 0)

    def write(index, carry):
        tile = amp_id[index] >> 8

        def first(other, value):
            return value + fock_scalar[tile, amp_id[other] >> 8] * tiles[slot_rows(other), :]

        value = lax.fori_loop(0, n_amp, first, sums[slot_rows(index), :])
        turned = pltpu.roll(value, TS, 1)
        odd = tile & 1
        lanes = pl.ds(pl.multiple_of((tile >> 1) * LANES, LANES), LANES)
        side = iota((HALF, LANES), 1) // TS == odd
        is_odd = iota((HALF, LANES), 0) * 0 + odd == 1
        upper = jnp.where(is_odd, turned, value)
        lower = jnp.where(is_odd, value, turned)
        out[0, :HALF, lanes] = jnp.where(side, upper, out[0, :HALF, lanes])
        out[0, HALF:, lanes] = jnp.where(side, lower, out[0, HALF:, lanes])
        return carry

    lax.fori_loop(0, n_amp, write, 0)


def local(
    amplitudes, pp_integrals, hole_fock, tile_pattern, integral_pattern, tile_extent, tile_owner
):
    rows, cols = lax.axis_size("row"), lax.axis_size("col")
    groups = tile_extent.shape[0]
    arguments = (
        amplitudes,
        pp_integrals,
        hole_fock,
        tile_pattern,
        integral_pattern,
        tile_extent,
        tile_owner,
    )
    row_tiles, integral_tiles = tile_pattern.shape[0], integral_pattern.shape[0]
    if groups != rows or integral_tiles % groups or rows & (rows - 1) or cols & (cols - 1):
        return dense(*arguments)
    lay = Layout(rows, cols, row_tiles, integral_tiles, groups)
    devices = rows * cols

    def smem(shape):
        return pltpu.SMEM(shape, jnp.int32)

    in_smem = pl.BlockSpec(memory_space=pltpu.SMEM)
    in_vmem = pl.BlockSpec(memory_space=pltpu.VMEM)
    params = pltpu.CompilerParams(vmem_limit_bytes=32 * 2**20)
    packed_shape = (ROW_SLOTS * HALF, LANES)

    packed, mine = pl.pallas_call(
        lambda *refs: pack_kernel(lay, *refs),
        out_shape=(
            jax.ShapeDtypeStruct(packed_shape, jnp.float32),
            jax.ShapeDtypeStruct((devices, 1, lay.width), jnp.int32),
        ),
        in_specs=[in_smem] * 3 + [in_vmem] * 5,
        out_specs=(in_vmem, in_vmem),
        scratch_shapes=[
            pltpu.VMEM((LANES, TS), jnp.float32),
            smem(((row_tiles + integral_tiles) * groups + 1,)),
        ],
        compiler_params=params,
        name="pack_tiles",
    )(
        tile_pattern.T,
        integral_pattern.T,
        tile_extent,
        tile_pattern.T,
        integral_pattern.T,
        tile_owner,
        amplitudes,
        pp_integrals,
    )
    shares = [packed]
    for k in range(1, rows):
        shares.append(lax.ppermute(packed, "row", [(i, i ^ k) for i in range(rows)]))
    info = lax.all_to_all(mine, ("row", "col"), split_axis=0, concat_axis=0, tiled=True)

    level = pl.pallas_call(
        lambda *refs: check_kernel(lay, *refs),
        out_shape=jax.ShapeDtypeStruct((1,), jnp.int32),
        in_specs=[in_vmem],
        out_specs=in_smem,
        compiler_params=params,
        name="check_slots",
    )(info)

    def forward(slots, info, *shares):
        message = (slots * HALF, LANES)
        messages = pl.pallas_call(
            lambda *refs: forward_kernel(lay, slots, *refs),
            out_shape=[jax.ShapeDtypeStruct(message, jnp.float32)] * cols,
            in_specs=[in_smem] + [in_vmem] * rows,
            out_specs=[in_vmem] * cols,
            scratch_shapes=[
                pltpu.VMEM((cols,) + message, jnp.float32),
                smem((cols * groups + 1,)),
                smem((rows, cols * slots + row_tiles + 1)),
            ],
            compiler_params=params,
            name="forward_tiles",
        )(info, *shares)
        return [messages[0]] + [
            lax.ppermute(messages[k], "col", [(i, i ^ k) for i in range(cols)])
            for k in range(1, cols)
        ]

    received = forward(COL_SLOTS[0], info, *shares)

    def finish(info, received, shares, arguments):
        return pl.pallas_call(
            lambda *refs: finish_kernel(lay, *refs),
            out_shape=jax.ShapeDtypeStruct((1, TS, rows * row_tiles * TS), jnp.float32),
            in_specs=[in_smem] * 3 + [in_vmem] * (1 + rows + cols),
            out_specs=in_vmem,
            scratch_shapes=[
                smem((rows * row_tiles + 1,)),
                smem((rows * integral_tiles + 1,)),
                smem((cols,)),
                pltpu.VMEM((rows * (row_tiles + 1) * HALF, LANES), jnp.float32),
                pltpu.VMEM((rows * integral_tiles * HALF, LANES), jnp.float32),
                pltpu.VMEM((rows * (row_tiles + 1) * HALF, LANES), jnp.float32),
                pltpu.VMEM((cols,) + received[0].shape, jnp.float32),
            ],
            compiler_params=params,
            name="finish_residual",
        )(info, arguments[5], arguments[2], arguments[2], *shares, *received)

    def more_slots(info, received, shares, arguments):
        return finish(info, forward(COL_SLOTS[1], info, *shares), shares, arguments)

    def all_tiles(info, received, shares, arguments):
        return dense(*arguments)

    return lax.switch(
        level[0], (finish, more_slots, all_tiles), info, received, tuple(shares), arguments
    )


def solution(mesh):
    placed = (
        P("row", "col"),
        P("row", "col"),
        P(),
        P("row", "col"),
        P("row", "col"),
        P("col"),
        P("col", None),
    )
    return jax.shard_map(
        local, mesh=mesh, in_specs=placed, out_specs=P(("row", "col"), None, None), check_vma=False
    )
```

```python
import jax
import jax.numpy as jnp
from jax import lax
from jax.experimental import pallas as pl
from jax.experimental.pallas import tpu as pltpu
from jax.sharding import PartitionSpec as P

NO = 64
TS = 64
HALF = TS // 2
LANES = 2 * TS
ROW_SLOTS = 16
COL_SLOTS = (2, 4)
HIGHEST = lax.Precision.HIGHEST


def gather_exchange(values, axis):
    count = lax.axis_size(axis)
    copies = jnp.broadcast_to(values[None], (count,) + values.shape)
    return lax.all_to_all(copies, axis, split_axis=0, concat_axis=0)


def occupied_term(moved, hole_fock):
    shape_in = moved.shape
    paired = moved.reshape(NO, NO, shape_in[1] * shape_in[2])
    result = jnp.einsum("ik,kjc->ijc", hole_fock, paired, precision=HIGHEST)
    result = result + jnp.einsum("jk,ikc->ijc", hole_fock, paired, precision=HIGHEST)
    return result.reshape(shape_in)


def dense(
    amplitudes, pp_integrals, hole_fock, tile_pattern, integral_pattern, tile_extent, tile_owner
):
    row_count, col_count = amplitudes.shape
    groups = tile_extent.shape[0]
    col_keep = (lax.broadcasted_iota(jnp.int32, (groups, TS), 1) < tile_extent[:, None]).astype(
        jnp.float32
    )
    pattern_float = tile_pattern.astype(jnp.float32)
    keep_mask = (
        jnp.repeat(jnp.repeat(pattern_float, TS, 0), TS, 1) * col_keep.reshape(col_count)[None, :]
    )
    masked = amplitudes * keep_mask
    integrals = pp_integrals * jnp.repeat(
        jnp.repeat(integral_pattern.astype(jnp.float32), TS, 0), TS, 1
    )
    owner_list = tile_owner[0]
    slot_count = groups // lax.axis_size("row")
    my_tiles = lax.dynamic_slice_in_dim(owner_list, lax.axis_index("row") * slot_count, slot_count)

    def ordered(values):
        return jnp.take(values.reshape(values.shape[0], groups, TS), owner_list, axis=1)

    pattern_sent = jnp.take(pattern_float, owner_list, axis=1)
    column_block = gather_exchange(integrals, "row")
    column_block = column_block.reshape(-1, col_count)
    row_block = gather_exchange(masked, "col")
    row_block = jnp.transpose(row_block, (1, 0, 2)).reshape(row_count, -1)
    ladder = jnp.dot(
        row_block, column_block, precision=HIGHEST, preferred_element_type=jnp.float32
    )
    moved_amps, moved_ladder, moved_pattern = (
        lax.all_to_all(ordered(masked), "row", split_axis=1, concat_axis=0, tiled=True),
        lax.all_to_all(ordered(ladder), "row", split_axis=1, concat_axis=0, tiled=True),
        lax.all_to_all(pattern_sent, "row", split_axis=1, concat_axis=0, tiled=True),
    )
    occupied = occupied_term(moved_amps, hole_fock)
    extents = jnp.take(tile_extent, my_tiles)
    extent_keep = (lax.broadcasted_iota(jnp.int32, (slot_count, TS), 1) < extents[:, None]).astype(
        jnp.float32
    )
    final_keep = jnp.repeat(moved_pattern, TS, 0)[:, :, None] * extent_keep[None, :, :]
    full = (moved_ladder + occupied) * final_keep
    return jnp.transpose(full, (1, 2, 0))


class Layout:
    def __init__(self, rows, cols, row_tiles, integral_tiles, groups):
        self.rows, self.cols, self.groups = rows, cols, groups
        self.row_tiles, self.integral_tiles = row_tiles, integral_tiles
        self.integral_at = groups * row_tiles
        self.owner_at = self.integral_at + groups * integral_tiles
        self.count_at = self.owner_at + groups
        self.width = -(-(self.count_at + 1) // 128) * 128

    def amp(self, info, row, tile, col, local):
        return info[row * self.cols + col, 0, local * self.row_tiles + tile]

    def integral(self, info, row, tile, col, local):
        return info[row * self.cols + col, 0, self.integral_at + local * self.integral_tiles + tile]

    def owner(self, info, row, col):
        return info[col, 0, self.owner_at + row]


def present(code):
    return jnp.minimum(code, 1)


def slot_rows(slot):
    return pl.ds(pl.multiple_of(slot * HALF, HALF), HALF)


def load_transposed(source, turn, tile, local, extent):
    lanes = pl.multiple_of((local >> 1) * LANES, LANES)
    rows = pl.multiple_of(tile * TS, TS)
    turn[...] = source[pl.ds(rows, TS), pl.ds(lanes, LANES)].T
    start = pl.multiple_of((local & 1) * TS, TS)
    upper = turn[pl.ds(start, HALF), :]
    lower = turn[pl.ds(start + HALF, HALF), :]
    if extent is not None:
        position = lax.broadcasted_iota(jnp.int32, (HALF, TS), 0)
        upper = jnp.where(position < extent, upper, 0.0)
        lower = jnp.where(position + HALF < extent, lower, 0.0)
    return jnp.concatenate([upper, lower], axis=1)


def unfold(packed):
    return jnp.concatenate([packed[:, :TS], packed[:, TS:]], axis=0)


def fold(tile):
    return jnp.concatenate([tile[:HALF], tile[HALF:]], axis=1)


def iota(shape, axis):
    return lax.broadcasted_iota(jnp.int32, shape, axis)


def pack_kernel(
    lay, amp_bits, int_bits, extent, amp_vec, int_vec, owner_vec, amps, ints, packed, info_out, turn, items
):
    pieces = [amp_vec[q : q + 1, :] for q in range(lay.groups)]
    pieces += [int_vec[q : q + 1, :] for q in range(lay.groups)]
    pieces += [owner_vec[...], jnp.zeros((1, lay.width - lay.count_at), jnp.int32)]
    entries = jnp.concatenate(pieces, axis=1).astype(jnp.float32)
    lane = iota((1, lay.width), 1)
    bits = jnp.where(lane < lay.owner_at, entries, 0.0)
    ahead = (iota((lay.width, lay.width), 0) <= iota((lay.width, lay.width), 1)).astype(jnp.float32)
    ranks = jnp.dot(
        jnp.broadcast_to(bits, (8, lay.width)), ahead, preferred_element_type=jnp.float32
    )[:1]
    row = jnp.where(lane < lay.owner_at, bits * ranks, entries)
    row = jnp.where(lane == lay.count_at, ranks, row).astype(jnp.int32)
    info_out[...] = jnp.broadcast_to(row[None], info_out.shape)
    n_amp = jnp.int32(0)
    for local in range(lay.groups):
        for tile in range(lay.row_tiles):
            items[n_amp] = tile * 256 + local
            n_amp += amp_bits[local, tile]
    n_all = n_amp
    for local in range(lay.groups):
        for tile in range(lay.integral_tiles):
            items[n_all] = tile * 256 + local
            n_all += int_bits[local, tile]

    def place(source, with_extent):
        def body(slot, carry):
            item = items[slot]
            local, tile = item & 255, item >> 8
            packed[slot_rows(slot), :] = load_transposed(
                source, turn, tile, local, extent[local] if with_extent else None
            )
            return carry

        return body

    n_amp = jnp.minimum(n_amp, ROW_SLOTS)
    n_all = jnp.minimum(n_all, ROW_SLOTS)
    lax.fori_loop(0, n_amp, place(amps, True), 0)
    lax.fori_loop(n_amp, n_all, place(ints, False), 0)


def check_kernel(lay, info, result):
    codes = info[:, 0, :]
    here = jnp.minimum(codes, 1).astype(jnp.float32)
    lane = iota((1, lay.width), 1)
    contract = (((1,), (1,)), ((), ()))

    def field(start, length, block):
        shift = (lay.width - start) % lay.width
        moved = pltpu.roll(here, shift, 1) if shift else here
        return jnp.where(lane < length, moved, 0.0).reshape(lay.rows, lay.cols, lay.width)[block]

    shared = None
    for row in range(lay.rows):
        stack = jnp.concatenate(
            [field(q * lay.row_tiles, lay.row_tiles, row) for q in range(lay.groups)], axis=0
        )
        term = lax.dot_general(stack, stack, contract, preferred_element_type=jnp.float32)
        shared = term if shared is None else shared + term
    total = lay.groups * lay.cols
    tiles = lay.rows * lay.integral_tiles
    at, to = iota((total, tiles), 0), iota((total, tiles), 1)
    order = (at == (to % lay.groups) * lay.cols + to // lay.groups).astype(jnp.float32)
    shared = jnp.dot(shared, order, preferred_element_type=jnp.float32)
    at, to = iota((total, tiles), 0), iota((total, tiles), 1)
    own = to == (at % lay.cols) * lay.groups + at // lay.cols
    shared = jnp.where(own, 0.0, shared)
    counts = None
    for row in range(lay.rows):
        stack = jnp.concatenate(
            [
                field(lay.integral_at + q * lay.integral_tiles, lay.integral_tiles, row)
                for q in range(lay.groups)
            ],
            axis=0,
        )
        wide = stack[:, : lay.integral_tiles]
        mine = wide * shared[:, row * lay.integral_tiles : (row + 1) * lay.integral_tiles]
        at, to = iota((lay.integral_tiles, 128), 0), iota((lay.integral_tiles, 128), 1)
        group = (at // lay.groups == to).astype(jnp.float32)
        term = jnp.dot(mine, group, preferred_element_type=jnp.float32)
        counts = term if counts is None else jnp.maximum(counts, term)
    most = jnp.max(counts)
    used = jnp.max(jnp.where(lane == lay.count_at, codes, 0))
    level = jnp.where(most > COL_SLOTS[0], 1, 0)
    result[0] = jnp.where((most > COL_SLOTS[1]) | (used > ROW_SLOTS), 2, level)


def forward_kernel(lay, slots, info, *refs):
    packed, (out, pairs, lists) = refs[: lay.rows], refs[lay.rows :]
    row, col = lax.axis_index("row"), lax.axis_index("col")
    base = col * lay.groups
    int_row, int_tile = base // lay.integral_tiles, base % lay.integral_tiles
    n_pairs = jnp.int32(0)
    for target in range(lay.cols):
        wanted = lay.owner(info, row, target)
        for local in range(lay.groups):
            pairs[n_pairs] = target * 256 + local
            hit = present(lay.integral(info, int_row, int_tile + local, target, wanted))
            n_pairs += jnp.where((target == col) & (wanted == local), 0, hit)

    def scan(index, carry):
        counts, previous, slot = carry
        pair = pairs[index]
        local, target = pair & 255, pair >> 8
        wanted = lay.owner(info, row, target)
        slot = jnp.where(target == previous, slot, 0)
        updated = []
        for k in range(lay.rows):
            count = counts[k]
            for tile in range(lay.row_tiles):
                code = lay.amp(info, row ^ k, tile, col, local)
                hit = present(code * lay.amp(info, row ^ k, tile, target, wanted))
                lists[k, count] = ((target * 256) + jnp.minimum(slot, 255)) * 256 + code - 1
                count += hit
                slot += hit
            updated.append(jnp.minimum(count, lay.cols * slots))
        return tuple(updated), target, slot

    zero = jnp.int32(0)
    counts, _, _ = lax.fori_loop(0, n_pairs, scan, ((zero,) * lay.rows, jnp.int32(-1), zero))
    for k in range(lay.rows):

        def send(index, carry, k=k):
            item = lists[k, index]
            source, slot, target = item & 255, (item >> 8) & 255, item >> 16

            @pl.when((slot < slots) & (source < ROW_SLOTS))
            def _():
                out[target, slot_rows(slot), :] = packed[k][slot_rows(source), :]

            return carry

        lax.fori_loop(0, counts[k], send, 0)


def occupied_kernel(lay, info, extent, fock_scalar, fock, *refs):
    packed = refs[: lay.rows]
    out, todo, amp_id, int_id, next_slot, tiles, sums = refs[lay.rows :]
    row, col = lax.axis_index("row"), lax.axis_index("col")
    local = lay.owner(info, row, col)
    limit = extent[local]
    out[...] = jnp.zeros_like(out)
    for source in range(lay.cols):
        next_slot[source] = 0
    n_amp = jnp.int32(0)
    n_int = jnp.int32(0)
    for k in range(lay.rows):
        first = n_amp
        for tile in range(lay.row_tiles):
            code = lay.amp(info, row ^ k, tile, col, local)
            amp_id[n_amp] = ((row ^ k) * lay.row_tiles + tile) * 256 + jnp.clip(
                code - 1, 0, ROW_SLOTS - 1
            )
            n_amp += present(code)

        def take_amp(index, carry, k=k):
            tiles[slot_rows(index), :] = packed[k][slot_rows(amp_id[index] & 255), :]
            return carry

        lax.fori_loop(first, n_amp, take_amp, 0)
        for tile in range(lay.integral_tiles):
            code = lay.integral(info, row ^ k, tile, col, local)
            int_id[n_int] = (((row ^ k) * lay.integral_tiles + tile) * 256 + k) * 256 + jnp.clip(
                code - 1, 0, ROW_SLOTS - 1
            )
            n_int += present(code)

    blank = jnp.zeros((TS, TS), jnp.float32)
    both = jnp.concatenate(
        [
            jnp.concatenate([fock[...], blank], axis=1),
            jnp.concatenate([blank, fock[...]], axis=1),
        ],
        axis=0,
    )
    chunk = 4 * HALF

    def second(index, carry):
        rows = pl.ds(pl.multiple_of(index * chunk, chunk), chunk)
        sums[rows, :] = lax.dot_general(
            tiles[rows, :],
            both,
            (((1,), (1,)), ((), ())),
            precision=HIGHEST,
            preferred_element_type=jnp.float32,
        )
        return carry

    lax.fori_loop(0, (n_amp + 3) >> 2, second, 0)

    def ladder(which, listed):
        item = int_id[which]
        middle = item >> 16
        source, middle_local = middle // lay.groups, middle % lay.groups
        own = (source == col) & (middle_local == local)
        own_row = middle // lay.integral_tiles

        for k in range(lay.rows):

            @pl.when(own & (row ^ k == own_row))
            def _():
                integral = unfold(packed[k][slot_rows(item & 255), :])

                def diagonal(index, carry):
                    product = jnp.dot(
                        integral,
                        unfold(tiles[slot_rows(index), :]),
                        precision=HIGHEST,
                        preferred_element_type=jnp.float32,
                    )
                    product = jnp.where(iota((TS, TS), 0) < limit, product, 0.0)
                    sums[slot_rows(index), :] += fold(product)
                    return carry

                lax.fori_loop(0, n_amp, diagonal, 0)

        def arriving(index, listed):
            tile = amp_id[index] >> 8
            code = lay.amp(info, tile // lay.row_tiles, tile % lay.row_tiles, source, middle_local)
            slot = next_slot[source]
            todo[2 * listed] = (tile * 256 + source) * 256 + jnp.minimum(slot, 255)
            todo[2 * listed + 1] = item & 65535
            hit = present(code)
            next_slot[source] = slot + hit
            return jnp.minimum(listed + hit, lay.cols * COL_SLOTS[1])

        return lax.fori_loop(0, jnp.where(own, 0, n_amp), arriving, listed)

    todo[2 * lay.cols * COL_SLOTS[1] + 2] = lax.fori_loop(0, n_int, ladder, jnp.int32(0))
    todo[2 * lay.cols * COL_SLOTS[1] + 3] = limit

    def write(index, carry):
        tile = amp_id[index] >> 8

        def first(other, value):
            return value + fock_scalar[tile, amp_id[other] >> 8] * tiles[slot_rows(other), :]

        value = lax.fori_loop(0, n_amp, first, sums[slot_rows(index), :])
        turned = pltpu.roll(value, TS, 1)
        odd = tile & 1
        lanes = pl.ds(pl.multiple_of((tile >> 1) * LANES, LANES), LANES)
        side = iota((HALF, LANES), 1) // TS == odd
        is_odd = iota((HALF, LANES), 0) * 0 + odd == 1
        upper = jnp.where(is_odd, turned, value)
        lower = jnp.where(is_odd, value, turned)
        out[0, :HALF, lanes] = jnp.where(side, upper, out[0, :HALF, lanes])
        out[0, HALF:, lanes] = jnp.where(side, lower, out[0, HALF:, lanes])
        return carry

    lax.fori_loop(0, n_amp, write, 0)


def ladder_kernel(lay, todo, received, partial, *refs):
    packed, (out, integral) = refs[: lay.rows], refs[lay.rows :]
    out[...] = partial[...]
    limit = todo[2 * lay.cols * COL_SLOTS[1] + 3]

    def add(index, carry):
        item, where = todo[2 * index], todo[2 * index + 1]
        slot, source, tile = item & 255, (item >> 8) & 255, item >> 16
        for k in range(lay.rows):

            @pl.when(where >> 8 == k)
            def _():
                integral[...] = packed[k][slot_rows(where & 255), :]

        product = jnp.dot(
            unfold(integral[...]),
            unfold(received[source, slot_rows(slot), :]),
            precision=HIGHEST,
            preferred_element_type=jnp.float32,
        )
        product = jnp.where(iota((TS, TS), 0) < limit, product, 0.0)
        side = iota((TS, LANES), 1) // TS == tile & 1
        lanes = pl.ds(pl.multiple_of((tile >> 1) * LANES, LANES), LANES)
        out[0, :, lanes] += jnp.where(side, jnp.concatenate([product, product], axis=1), 0.0)
        return carry

    lax.fori_loop(0, todo[2 * lay.cols * COL_SLOTS[1] + 2], add, 0)


def local(
    amplitudes, pp_integrals, hole_fock, tile_pattern, integral_pattern, tile_extent, tile_owner
):
    rows, cols = lax.axis_size("row"), lax.axis_size("col")
    groups = tile_extent.shape[0]
    arguments = (
        amplitudes,
        pp_integrals,
        hole_fock,
        tile_pattern,
        integral_pattern,
        tile_extent,
        tile_owner,
    )
    row_tiles, integral_tiles = tile_pattern.shape[0], integral_pattern.shape[0]
    if groups != rows or integral_tiles % groups or rows & (rows - 1):
        return dense(*arguments)
    lay = Layout(rows, cols, row_tiles, integral_tiles, groups)
    devices = rows * cols

    def smem(shape):
        return pltpu.SMEM(shape, jnp.int32)

    in_smem = pl.BlockSpec(memory_space=pltpu.SMEM)
    in_vmem = pl.BlockSpec(memory_space=pltpu.VMEM)
    params = pltpu.CompilerParams(vmem_limit_bytes=32 * 2**20)
    packed_shape = (ROW_SLOTS * HALF, LANES)

    packed, mine = pl.pallas_call(
        lambda *refs: pack_kernel(lay, *refs),
        out_shape=(
            jax.ShapeDtypeStruct(packed_shape, jnp.float32),
            jax.ShapeDtypeStruct((devices, 1, lay.width), jnp.int32),
        ),
        in_specs=[in_smem] * 3 + [in_vmem] * 5,
        out_specs=(in_vmem, in_vmem),
        scratch_shapes=[
            pltpu.VMEM((LANES, TS), jnp.float32),
            smem(((row_tiles + integral_tiles) * groups + 1,)),
        ],
        compiler_params=params,
        name="pack_tiles",
    )(
        tile_pattern.T,
        integral_pattern.T,
        tile_extent,
        tile_pattern.T,
        integral_pattern.T,
        tile_owner,
        amplitudes,
        pp_integrals,
    )
    shares = [packed]
    for k in range(1, rows):
        shares.append(lax.ppermute(packed, "row", [(i, i ^ k) for i in range(rows)]))
    info = lax.all_to_all(mine, ("row", "col"), split_axis=0, concat_axis=0, tiled=True)

    level = pl.pallas_call(
        lambda *refs: check_kernel(lay, *refs),
        out_shape=jax.ShapeDtypeStruct((1,), jnp.int32),
        in_specs=[in_vmem],
        out_specs=in_smem,
        compiler_params=params,
        name="check_slots",
    )(info)

    def forward(slots, info, *shares):
        col_send = pl.pallas_call(
            lambda *refs: forward_kernel(lay, slots, *refs),
            out_shape=jax.ShapeDtypeStruct((cols, slots * HALF, LANES), jnp.float32),
            in_specs=[in_smem] + [in_vmem] * rows,
            out_specs=in_vmem,
            scratch_shapes=[
                smem((cols * groups + 1,)),
                smem((rows, cols * slots + row_tiles + 1)),
            ],
            compiler_params=params,
            name="forward_tiles",
        )(info, *shares)
        return lax.all_to_all(col_send, "col", split_axis=0, concat_axis=0, tiled=True)

    received = forward(COL_SLOTS[0], info, *shares)

    out_shape = (1, TS, rows * row_tiles * TS)
    all_tiles_rows = rows * (row_tiles + 1) * HALF
    partial, todo = pl.pallas_call(
        lambda *refs: occupied_kernel(lay, *refs),
        out_shape=(
            jax.ShapeDtypeStruct(out_shape, jnp.float32),
            jax.ShapeDtypeStruct((2 * cols * COL_SLOTS[1] + 4,), jnp.int32),
        ),
        in_specs=[in_smem] * 3 + [in_vmem] * (1 + rows),
        out_specs=(in_vmem, in_smem),
        scratch_shapes=[
            smem((rows * row_tiles + 1,)),
            smem((rows * integral_tiles + 1,)),
            smem((cols,)),
            pltpu.VMEM((all_tiles_rows, LANES), jnp.float32),
            pltpu.VMEM((all_tiles_rows, LANES), jnp.float32),
        ],
        compiler_params=params,
        name="occupied_terms",
    )(info, tile_extent, hole_fock, hole_fock, *shares)

    def finish(info, received, todo, partial, shares, arguments):
        return pl.pallas_call(
            lambda *refs: ladder_kernel(lay, *refs),
            out_shape=jax.ShapeDtypeStruct(out_shape, jnp.float32),
            in_specs=[in_smem] + [in_vmem] * (2 + rows),
            out_specs=in_vmem,
            scratch_shapes=[pltpu.VMEM((HALF, LANES), jnp.float32)],
            compiler_params=params,
            name="ladder_terms",
        )(todo, received, partial, *shares)

    def more_slots(info, received, todo, partial, shares, arguments):
        received = forward(COL_SLOTS[1], info, *shares)
        return finish(info, received, todo, partial, shares, arguments)

    def all_tiles(info, received, todo, partial, shares, arguments):
        return dense(*arguments)

    return lax.switch(
        level[0],
        (finish, more_slots, all_tiles),
        info,
        received,
        todo,
        partial,
        tuple(shares),
        arguments,
    )


def solution(mesh):
    placed = (
        P("row", "col"),
        P("row", "col"),
        P(),
        P("row", "col"),
        P("row", "col"),
        P("col"),
        P("col", None),
    )
    return jax.shard_map(
        local, mesh=mesh, in_specs=placed, out_specs=P(("row", "col"), None, None), check_vma=False
    )
```

```python
import jax
import jax.numpy as jnp
from jax import lax
from jax.experimental import pallas as pl
from jax.experimental.pallas import tpu as pltpu
from jax.sharding import PartitionSpec as P

NO = 64
TS = 64
HALF = TS // 2
LANES = 2 * TS
ROW_SLOTS = 16
COL_SLOTS = (2, 4)
HIGHEST = lax.Precision.HIGHEST


def gather_exchange(values, axis):
    count = lax.axis_size(axis)
    copies = jnp.broadcast_to(values[None], (count,) + values.shape)
    return lax.all_to_all(copies, axis, split_axis=0, concat_axis=0)


def occupied_term(moved, hole_fock):
    shape_in = moved.shape
    paired = moved.reshape(NO, NO, shape_in[1] * shape_in[2])
    result = jnp.einsum("ik,kjc->ijc", hole_fock, paired, precision=HIGHEST)
    result = result + jnp.einsum("jk,ikc->ijc", hole_fock, paired, precision=HIGHEST)
    return result.reshape(shape_in)


def dense(
    amplitudes, pp_integrals, hole_fock, tile_pattern, integral_pattern, tile_extent, tile_owner
):
    row_count, col_count = amplitudes.shape
    groups = tile_extent.shape[0]
    col_keep = (lax.broadcasted_iota(jnp.int32, (groups, TS), 1) < tile_extent[:, None]).astype(
        jnp.float32
    )
    pattern_float = tile_pattern.astype(jnp.float32)
    keep_mask = (
        jnp.repeat(jnp.repeat(pattern_float, TS, 0), TS, 1) * col_keep.reshape(col_count)[None, :]
    )
    masked = amplitudes * keep_mask
    integrals = pp_integrals * jnp.repeat(
        jnp.repeat(integral_pattern.astype(jnp.float32), TS, 0), TS, 1
    )
    owner_list = tile_owner[0]
    slot_count = groups // lax.axis_size("row")
    my_tiles = lax.dynamic_slice_in_dim(owner_list, lax.axis_index("row") * slot_count, slot_count)

    def ordered(values):
        return jnp.take(values.reshape(values.shape[0], groups, TS), owner_list, axis=1)

    pattern_sent = jnp.take(pattern_float, owner_list, axis=1)
    column_block = gather_exchange(integrals, "row")
    column_block = column_block.reshape(-1, col_count)
    row_block = gather_exchange(masked, "col")
    row_block = jnp.transpose(row_block, (1, 0, 2)).reshape(row_count, -1)
    ladder = jnp.dot(
        row_block, column_block, precision=HIGHEST, preferred_element_type=jnp.float32
    )
    moved_amps, moved_ladder, moved_pattern = (
        lax.all_to_all(ordered(masked), "row", split_axis=1, concat_axis=0, tiled=True),
        lax.all_to_all(ordered(ladder), "row", split_axis=1, concat_axis=0, tiled=True),
        lax.all_to_all(pattern_sent, "row", split_axis=1, concat_axis=0, tiled=True),
    )
    occupied = occupied_term(moved_amps, hole_fock)
    extents = jnp.take(tile_extent, my_tiles)
    extent_keep = (lax.broadcasted_iota(jnp.int32, (slot_count, TS), 1) < extents[:, None]).astype(
        jnp.float32
    )
    final_keep = jnp.repeat(moved_pattern, TS, 0)[:, :, None] * extent_keep[None, :, :]
    full = (moved_ladder + occupied) * final_keep
    return jnp.transpose(full, (1, 2, 0))


class Layout:
    def __init__(self, rows, cols, row_tiles, integral_tiles, groups):
        self.rows, self.cols, self.groups = rows, cols, groups
        self.row_tiles, self.integral_tiles = row_tiles, integral_tiles
        self.integral_at = groups * row_tiles
        self.owner_at = self.integral_at + groups * integral_tiles
        self.count_at = self.owner_at + groups
        self.items_at = self.count_at + 2
        self.width = -(-(self.items_at + ROW_SLOTS) // 128) * 128

    def amp(self, info, row, tile, col, local):
        return info[row * self.cols + col, 0, local * self.row_tiles + tile]

    def integral(self, info, row, tile, col, local):
        return info[row * self.cols + col, 0, self.integral_at + local * self.integral_tiles + tile]

    def owner(self, info, row, col):
        return info[col, 0, self.owner_at + row]


def present(code):
    return jnp.minimum(code, 1)


def slot_rows(slot):
    return pl.ds(pl.multiple_of(slot * HALF, HALF), HALF)


def unfold(packed):
    return jnp.concatenate([packed[:, :TS], packed[:, TS:]], axis=0)


def fold(tile):
    return jnp.concatenate([tile[:HALF], tile[HALF:]], axis=1)


def iota(shape, axis):
    return lax.broadcasted_iota(jnp.int32, shape, axis)


def pack_kernel(
    lay, amp_bits, int_bits, extent, amp_vec, int_vec, owner_vec, amps, ints, packed, info_out, blocks, turn, items, limits, sems
):
    n_amp = jnp.int32(0)
    for local in range(lay.groups):
        for tile in range(lay.row_tiles):
            items[n_amp] = tile * 256 + local
            n_amp += amp_bits[local, tile]
    n_all = n_amp
    for local in range(lay.groups):
        for tile in range(lay.integral_tiles):
            items[n_all] = tile * 256 + local
            n_all += int_bits[local, tile]
    some_amp = jnp.minimum(n_amp, ROW_SLOTS)
    some = jnp.minimum(n_all, ROW_SLOTS)

    def fetch(source, slot):
        item = items[slot]
        rows = pl.ds(pl.multiple_of((item >> 8) * TS, TS), TS)
        lanes = pl.ds(pl.multiple_of(((item & 255) >> 1) * LANES, LANES), LANES)
        return pltpu.make_async_copy(source.at[rows, lanes], blocks.at[slot], sems.at[slot])

    def start_amp(slot, carry):
        fetch(amps, slot).start()
        limits[slot] = extent[items[slot] & 255]
        return carry

    def start_int(slot, carry):
        fetch(ints, slot).start()
        limits[slot] = TS
        return carry

    lax.fori_loop(0, some_amp, start_amp, 0)
    lax.fori_loop(some_amp, some, start_int, 0)
    pieces = [amp_vec[q : q + 1, :] for q in range(lay.groups)]
    pieces += [int_vec[q : q + 1, :] for q in range(lay.groups)]
    pieces += [owner_vec[...], jnp.zeros((1, lay.width - lay.count_at), jnp.int32)]
    entries = jnp.concatenate(pieces, axis=1).astype(jnp.float32)
    lane = iota((1, lay.width), 1)
    bits = jnp.where(lane < lay.owner_at, entries, 0.0)
    ahead = (iota((lay.width, lay.width), 0) <= iota((lay.width, lay.width), 1)).astype(jnp.float32)
    ranks = jnp.dot(
        jnp.broadcast_to(bits, (8, lay.width)), ahead, preferred_element_type=jnp.float32
    )[:1]
    row = jnp.where(lane < lay.owner_at, bits * ranks, entries).astype(jnp.int32)
    row = jnp.where(lane == lay.count_at, n_all, row)
    row = jnp.where(lane == lay.count_at + 1, n_amp, row)
    for slot in range(ROW_SLOTS):
        row = jnp.where(lane == lay.items_at + slot, items[slot], row)
    info_out[...] = jnp.broadcast_to(row[None], info_out.shape)

    def wait_amp(slot, carry):
        fetch(amps, slot).wait()
        return carry

    def wait_int(slot, carry):
        fetch(ints, slot).wait()
        return carry

    lax.fori_loop(0, some_amp, wait_amp, 0)
    lax.fori_loop(some_amp, some, wait_int, 0)
    position = iota((HALF, TS), 0)

    def place(index, carry):
        slots = [jnp.minimum(4 * index + j, some - 1) for j in range(4)]
        for j, slot in enumerate(slots):
            turn[j] = blocks[slot].T
        for j, slot in enumerate(slots):
            start = pl.multiple_of((items[slot] & 1) * TS, TS)
            upper = turn[j, pl.ds(start, HALF), :]
            lower = turn[j, pl.ds(start + HALF, HALF), :]
            upper = jnp.where(position < limits[slot], upper, 0.0)
            lower = jnp.where(position + HALF < limits[slot], lower, 0.0)
            packed[slot_rows(slot), :] = jnp.concatenate([upper, lower], axis=1)
        return carry

    lax.fori_loop(0, (some + 3) >> 2, place, 0)


def check_kernel(lay, info, result):
    codes = info[:, 0, :]
    here = jnp.minimum(codes, 1).astype(jnp.float32)
    lane = iota((1, lay.width), 1)
    contract = (((1,), (1,)), ((), ()))

    def field(start, length, block):
        shift = (lay.width - start) % lay.width
        moved = pltpu.roll(here, shift, 1) if shift else here
        return jnp.where(lane < length, moved, 0.0).reshape(lay.rows, lay.cols, lay.width)[block]

    shared = None
    for row in range(lay.rows):
        stack = jnp.concatenate(
            [field(q * lay.row_tiles, lay.row_tiles, row) for q in range(lay.groups)], axis=0
        )
        term = lax.dot_general(stack, stack, contract, preferred_element_type=jnp.float32)
        shared = term if shared is None else shared + term
    total = lay.groups * lay.cols
    tiles = lay.rows * lay.integral_tiles
    at, to = iota((total, tiles), 0), iota((total, tiles), 1)
    order = (at == (to % lay.groups) * lay.cols + to // lay.groups).astype(jnp.float32)
    shared = jnp.dot(shared, order, preferred_element_type=jnp.float32)
    at, to = iota((total, tiles), 0), iota((total, tiles), 1)
    own = to == (at % lay.cols) * lay.groups + at // lay.cols
    shared = jnp.where(own, 0.0, shared)
    counts = None
    for row in range(lay.rows):
        stack = jnp.concatenate(
            [
                field(lay.integral_at + q * lay.integral_tiles, lay.integral_tiles, row)
                for q in range(lay.groups)
            ],
            axis=0,
        )
        wide = stack[:, : lay.integral_tiles]
        mine = wide * shared[:, row * lay.integral_tiles : (row + 1) * lay.integral_tiles]
        at, to = iota((lay.integral_tiles, 128), 0), iota((lay.integral_tiles, 128), 1)
        group = (at // lay.groups == to).astype(jnp.float32)
        term = jnp.dot(mine, group, preferred_element_type=jnp.float32)
        counts = term if counts is None else jnp.maximum(counts, term)
    most = jnp.max(counts)
    used = jnp.max(jnp.where(lane == lay.count_at, codes, 0))
    level = jnp.where(most > COL_SLOTS[0], 1, 0)
    result[0] = jnp.where((most > COL_SLOTS[1]) | (used > ROW_SLOTS), 2, level)


def forward_kernel(lay, slots, info, *refs):
    packed, (out, pairs, lists, counts) = refs[: lay.rows], refs[lay.rows :]
    row, col = lax.axis_index("row"), lax.axis_index("col")
    base = col * lay.groups
    int_row, int_tile = base // lay.integral_tiles, base % lay.integral_tiles
    n_pairs = jnp.int32(0)
    for target in range(lay.cols):
        wanted = lay.owner(info, row, target)
        for local in range(lay.groups):
            pairs[n_pairs] = (target * 256 + local) * 256 + wanted
            hit = present(lay.integral(info, int_row, int_tile + local, target, wanted))
            n_pairs += jnp.where((target == col) & (wanted == local), 0, hit)
    for local in range(lay.groups):
        counts[local] = 0
    for k in range(lay.rows):
        device = (row ^ k) * lay.cols + col

        def sort(slot, carry, k=k, device=device):
            item = info[device, 0, lay.items_at + slot]
            local = item & 255
            count = counts[local]
            lists[local, count] = ((item >> 8) * 256 + slot) * 256 + k
            counts[local] = count + 1
            return carry

        lax.fori_loop(
            0, jnp.minimum(info[device, 0, lay.count_at + 1], ROW_SLOTS), sort, 0
        )

    def scan(index, carry):
        previous, slot = carry
        pair = pairs[index]
        wanted, local, target = pair & 255, (pair >> 8) & 255, pair >> 16

        def per_tile(index, slot):
            item = lists[local, index]
            which, source, tile = item & 255, (item >> 8) & 255, item >> 16
            hit = present(lay.amp(info, row ^ which, tile, target, wanted))

            @pl.when((hit > 0) & (slot < slots))
            def _():
                for k in range(lay.rows):

                    @pl.when(which == k)
                    def _():
                        out[target, slot_rows(slot), :] = packed[k][slot_rows(source), :]

            return slot + hit

        slot = jnp.where(target == previous, slot, 0)
        return target, lax.fori_loop(0, counts[local], per_tile, slot)

    lax.fori_loop(0, n_pairs, scan, (jnp.int32(-1), jnp.int32(0)))


def occupied_kernel(lay, info, extent, fock_scalar, fock, *refs):
    packed = refs[: lay.rows]
    out, todo, amp_id, int_id, next_slot, tiles, sums = refs[lay.rows :]
    row, col = lax.axis_index("row"), lax.axis_index("col")
    local = lay.owner(info, row, col)
    limit = extent[local]
    out[...] = jnp.zeros_like(out)
    for source in range(lay.cols):
        next_slot[source] = 0
    n_amp = jnp.int32(0)
    n_int = jnp.int32(0)
    for k in range(lay.rows):
        first = n_amp
        for tile in range(lay.row_tiles):
            code = lay.amp(info, row ^ k, tile, col, local)
            amp_id[n_amp] = ((row ^ k) * lay.row_tiles + tile) * 256 + code
            n_amp += present(code)

        def take_amp(index, carry, k=k):
            slot = jnp.minimum((amp_id[index] & 255) - 1, ROW_SLOTS - 1)
            tiles[slot_rows(index), :] = packed[k][slot_rows(slot), :]
            return carry

        lax.fori_loop(first, n_amp, take_amp, 0)
        for tile in range(lay.integral_tiles):
            code = lay.integral(info, row ^ k, tile, col, local)
            int_id[n_int] = (((row ^ k) * lay.integral_tiles + tile) * 256 + k) * 256 + code
            n_int += present(code)
    for beyond in range(4):
        amp_id[n_amp + beyond] = 0
        tiles[slot_rows(n_amp + beyond), :] = jnp.zeros((HALF, LANES), jnp.float32)

    blank = jnp.zeros((TS, TS), jnp.float32)
    both = jnp.concatenate(
        [
            jnp.concatenate([fock[...], blank], axis=1),
            jnp.concatenate([blank, fock[...]], axis=1),
        ],
        axis=0,
    )
    chunk = 4 * HALF

    def second(index, carry):
        rows = pl.ds(pl.multiple_of(index * chunk, chunk), chunk)
        sums[rows, :] = lax.dot_general(
            tiles[rows, :],
            both,
            (((1,), (1,)), ((), ())),
            precision=HIGHEST,
            preferred_element_type=jnp.float32,
        )
        return carry

    lax.fori_loop(0, (n_amp + 3) >> 2, second, 0)

    def int_slot(item):
        return jnp.minimum((item & 255) - 1, ROW_SLOTS - 1)

    def ladder(which, listed):
        item = int_id[which]
        middle = item >> 16
        source, middle_local = middle // lay.groups, middle % lay.groups
        own = (source == col) & (middle_local == local)
        own_row = middle // lay.integral_tiles

        for k in range(lay.rows):

            @pl.when(own & (row ^ k == own_row))
            def _():
                integral = unfold(packed[k][slot_rows(int_slot(item)), :])

                def diagonal(index, carry):
                    pair = [unfold(tiles[slot_rows(2 * index + j), :]) for j in range(2)]
                    product = jnp.dot(
                        integral,
                        jnp.concatenate(pair, axis=1),
                        precision=HIGHEST,
                        preferred_element_type=jnp.float32,
                    )
                    product = jnp.where(iota((TS, LANES), 0) < limit, product, 0.0)
                    sums[slot_rows(2 * index), :] += fold(product[:, :TS])
                    sums[slot_rows(2 * index + 1), :] += fold(product[:, TS:])
                    return carry

                lax.fori_loop(0, (n_amp + 1) >> 1, diagonal, 0)

        def arriving(index, listed):
            tile = amp_id[index] >> 8
            code = lay.amp(info, tile // lay.row_tiles, tile % lay.row_tiles, source, middle_local)
            slot = next_slot[source]
            todo[2 * listed] = (tile * 256 + source) * 256 + jnp.minimum(slot, 255)
            todo[2 * listed + 1] = ((item >> 8) & 255) * 256 + int_slot(item)
            hit = present(code)
            next_slot[source] = slot + hit
            return jnp.minimum(listed + hit, lay.cols * COL_SLOTS[1])

        return lax.fori_loop(0, jnp.where(own, 0, n_amp), arriving, listed)

    todo[2 * lay.cols * COL_SLOTS[1] + 2] = lax.fori_loop(0, n_int, ladder, jnp.int32(0))
    todo[2 * lay.cols * COL_SLOTS[1] + 3] = limit

    def write(index, carry):
        tile = amp_id[index] >> 8

        def first(step, values):
            values = list(values)
            for j in range(4):
                other = 4 * step + j
                scale = fock_scalar[tile, amp_id[other] >> 8]
                values[j & 1] = values[j & 1] + scale * tiles[slot_rows(other), :]
            return tuple(values)

        start = (sums[slot_rows(index), :], jnp.zeros((HALF, LANES), jnp.float32))
        value, other = lax.fori_loop(0, (n_amp + 3) >> 2, first, start)
        value = value + other
        turned = pltpu.roll(value, TS, 1)
        odd = tile & 1
        lanes = pl.ds(pl.multiple_of((tile >> 1) * LANES, LANES), LANES)
        side = iota((HALF, LANES), 1) // TS == odd
        is_odd = iota((HALF, LANES), 0) * 0 + odd == 1
        upper = jnp.where(is_odd, turned, value)
        lower = jnp.where(is_odd, value, turned)
        out[0, :HALF, lanes] = jnp.where(side, upper, out[0, :HALF, lanes])
        out[0, HALF:, lanes] = jnp.where(side, lower, out[0, HALF:, lanes])
        return carry

    lax.fori_loop(0, n_amp, write, 0)


def ladder_kernel(lay, todo, received, partial, *refs):
    packed, (out, integral) = refs[: lay.rows], refs[lay.rows :]
    out[...] = partial[...]
    limit = todo[2 * lay.cols * COL_SLOTS[1] + 3]

    def add(index, carry):
        item, where = todo[2 * index], todo[2 * index + 1]
        slot, source, tile = item & 255, (item >> 8) & 255, item >> 16
        for k in range(lay.rows):

            @pl.when(where >> 8 == k)
            def _():
                integral[...] = packed[k][slot_rows(where & 255), :]

        product = jnp.dot(
            unfold(integral[...]),
            unfold(received[source, slot_rows(slot), :]),
            precision=HIGHEST,
            preferred_element_type=jnp.float32,
        )
        product = jnp.where(iota((TS, TS), 0) < limit, product, 0.0)
        side = iota((TS, LANES), 1) // TS == tile & 1
        lanes = pl.ds(pl.multiple_of((tile >> 1) * LANES, LANES), LANES)
        out[0, :, lanes] += jnp.where(side, jnp.concatenate([product, product], axis=1), 0.0)
        return carry

    lax.fori_loop(0, todo[2 * lay.cols * COL_SLOTS[1] + 2], add, 0)


def local(
    amplitudes, pp_integrals, hole_fock, tile_pattern, integral_pattern, tile_extent, tile_owner
):
    rows, cols = lax.axis_size("row"), lax.axis_size("col")
    groups = tile_extent.shape[0]
    arguments = (
        amplitudes,
        pp_integrals,
        hole_fock,
        tile_pattern,
        integral_pattern,
        tile_extent,
        tile_owner,
    )
    row_tiles, integral_tiles = tile_pattern.shape[0], integral_pattern.shape[0]
    if groups != rows or integral_tiles % groups or rows & (rows - 1):
        return dense(*arguments)
    lay = Layout(rows, cols, row_tiles, integral_tiles, groups)
    devices = rows * cols

    def smem(shape):
        return pltpu.SMEM(shape, jnp.int32)

    in_smem = pl.BlockSpec(memory_space=pltpu.SMEM)
    in_vmem = pl.BlockSpec(memory_space=pltpu.VMEM)
    params = pltpu.CompilerParams(vmem_limit_bytes=32 * 2**20)
    packed_shape = (ROW_SLOTS * HALF, LANES)

    packed, mine = pl.pallas_call(
        lambda *refs: pack_kernel(lay, *refs),
        out_shape=(
            jax.ShapeDtypeStruct(packed_shape, jnp.float32),
            jax.ShapeDtypeStruct((devices, 1, lay.width), jnp.int32),
        ),
        in_specs=[in_smem] * 3 + [in_vmem] * 3 + [pl.BlockSpec(memory_space=pl.ANY)] * 2,
        out_specs=(in_vmem, in_vmem),
        scratch_shapes=[
            pltpu.VMEM((ROW_SLOTS, TS, LANES), jnp.float32),
            pltpu.VMEM((4, LANES, TS), jnp.float32),
            smem(((row_tiles + integral_tiles) * groups + ROW_SLOTS,)),
            smem((ROW_SLOTS,)),
            pltpu.SemaphoreType.DMA((ROW_SLOTS,)),
        ],
        compiler_params=params,
        name="pack_tiles",
    )(
        tile_pattern.T,
        integral_pattern.T,
        tile_extent,
        tile_pattern.T,
        integral_pattern.T,
        tile_owner,
        amplitudes,
        pp_integrals,
    )
    shares = [packed]
    for k in range(1, rows):
        shares.append(lax.ppermute(packed, "row", [(i, i ^ k) for i in range(rows)]))
    info = lax.all_to_all(mine, ("row", "col"), split_axis=0, concat_axis=0, tiled=True)

    level = pl.pallas_call(
        lambda *refs: check_kernel(lay, *refs),
        out_shape=jax.ShapeDtypeStruct((1,), jnp.int32),
        in_specs=[in_vmem],
        out_specs=in_smem,
        compiler_params=params,
        name="check_slots",
    )(info)

    def forward(slots, info, *shares):
        col_send = pl.pallas_call(
            lambda *refs: forward_kernel(lay, slots, *refs),
            out_shape=jax.ShapeDtypeStruct((cols, slots * HALF, LANES), jnp.float32),
            in_specs=[in_smem] + [in_vmem] * rows,
            out_specs=in_vmem,
            scratch_shapes=[
                smem((cols * groups + 1,)),
                smem((groups, rows * ROW_SLOTS)),
                smem((groups,)),
            ],
            compiler_params=params,
            name="forward_tiles",
        )(info, *shares)
        return lax.all_to_all(col_send, "col", split_axis=0, concat_axis=0, tiled=True)

    received = forward(COL_SLOTS[0], info, *shares)

    out_shape = (1, TS, rows * row_tiles * TS)
    all_tiles_rows = rows * (row_tiles + 1) * HALF
    partial, todo = pl.pallas_call(
        lambda *refs: occupied_kernel(lay, *refs),
        out_shape=(
            jax.ShapeDtypeStruct(out_shape, jnp.float32),
            jax.ShapeDtypeStruct((2 * cols * COL_SLOTS[1] + 4,), jnp.int32),
        ),
        in_specs=[in_smem] * 3 + [in_vmem] * (1 + rows),
        out_specs=(in_vmem, in_smem),
        scratch_shapes=[
            smem((rows * row_tiles + 4,)),
            smem((rows * integral_tiles + 1,)),
            smem((cols,)),
            pltpu.VMEM((all_tiles_rows, LANES), jnp.float32),
            pltpu.VMEM((all_tiles_rows, LANES), jnp.float32),
        ],
        compiler_params=params,
        name="occupied_terms",
    )(info, tile_extent, hole_fock, hole_fock, *shares)

    def finish(info, received, todo, partial, shares, arguments):
        return pl.pallas_call(
            lambda *refs: ladder_kernel(lay, *refs),
            out_shape=jax.ShapeDtypeStruct(out_shape, jnp.float32),
            in_specs=[in_smem] + [in_vmem] * (2 + rows),
            out_specs=in_vmem,
            scratch_shapes=[pltpu.VMEM((HALF, LANES), jnp.float32)],
            compiler_params=params,
            name="ladder_terms",
        )(todo, received, partial, *shares)

    def more_slots(info, received, todo, partial, shares, arguments):
        received = forward(COL_SLOTS[1], info, *shares)
        return finish(info, received, todo, partial, shares, arguments)

    def all_tiles(info, received, todo, partial, shares, arguments):
        return dense(*arguments)

    return lax.switch(
        level[0],
        (finish, more_slots, all_tiles),
        info,
        received,
        todo,
        partial,
        tuple(shares),
        arguments,
    )


def solution(mesh):
    placed = (
        P("row", "col"),
        P("row", "col"),
        P(),
        P("row", "col"),
        P("row", "col"),
        P("col"),
        P("col", None),
    )
    return jax.shard_map(
        local, mesh=mesh, in_specs=placed, out_specs=P(("row", "col"), None, None), check_vma=False
    )
```

```python
import jax
import jax.numpy as jnp
from jax import lax
from jax.experimental import pallas as pl
from jax.experimental.pallas import tpu as pltpu
from jax.sharding import PartitionSpec as P

NO = 64
TS = 64
HALF = TS // 2
LANES = 2 * TS
ROW_SLOTS = 16
COL_SLOTS = (2, 4)
HIGHEST = lax.Precision.HIGHEST


def gather_exchange(values, axis):
    count = lax.axis_size(axis)
    copies = jnp.broadcast_to(values[None], (count,) + values.shape)
    return lax.all_to_all(copies, axis, split_axis=0, concat_axis=0)


def occupied_term(moved, hole_fock):
    shape_in = moved.shape
    paired = moved.reshape(NO, NO, shape_in[1] * shape_in[2])
    result = jnp.einsum("ik,kjc->ijc", hole_fock, paired, precision=HIGHEST)
    result = result + jnp.einsum("jk,ikc->ijc", hole_fock, paired, precision=HIGHEST)
    return result.reshape(shape_in)


def dense(
    amplitudes, pp_integrals, hole_fock, tile_pattern, integral_pattern, tile_extent, tile_owner
):
    row_count, col_count = amplitudes.shape
    groups = tile_extent.shape[0]
    col_keep = (lax.broadcasted_iota(jnp.int32, (groups, TS), 1) < tile_extent[:, None]).astype(
        jnp.float32
    )
    pattern_float = tile_pattern.astype(jnp.float32)
    keep_mask = (
        jnp.repeat(jnp.repeat(pattern_float, TS, 0), TS, 1) * col_keep.reshape(col_count)[None, :]
    )
    masked = amplitudes * keep_mask
    integrals = pp_integrals * jnp.repeat(
        jnp.repeat(integral_pattern.astype(jnp.float32), TS, 0), TS, 1
    )
    owner_list = tile_owner[0]
    slot_count = groups // lax.axis_size("row")
    my_tiles = lax.dynamic_slice_in_dim(owner_list, lax.axis_index("row") * slot_count, slot_count)

    def ordered(values):
        return jnp.take(values.reshape(values.shape[0], groups, TS), owner_list, axis=1)

    pattern_sent = jnp.take(pattern_float, owner_list, axis=1)
    column_block = gather_exchange(integrals, "row")
    column_block = column_block.reshape(-1, col_count)
    row_block = gather_exchange(masked, "col")
    row_block = jnp.transpose(row_block, (1, 0, 2)).reshape(row_count, -1)
    ladder = jnp.dot(
        row_block, column_block, precision=HIGHEST, preferred_element_type=jnp.float32
    )
    moved_amps, moved_ladder, moved_pattern = (
        lax.all_to_all(ordered(masked), "row", split_axis=1, concat_axis=0, tiled=True),
        lax.all_to_all(ordered(ladder), "row", split_axis=1, concat_axis=0, tiled=True),
        lax.all_to_all(pattern_sent, "row", split_axis=1, concat_axis=0, tiled=True),
    )
    occupied = occupied_term(moved_amps, hole_fock)
    extents = jnp.take(tile_extent, my_tiles)
    extent_keep = (lax.broadcasted_iota(jnp.int32, (slot_count, TS), 1) < extents[:, None]).astype(
        jnp.float32
    )
    final_keep = jnp.repeat(moved_pattern, TS, 0)[:, :, None] * extent_keep[None, :, :]
    full = (moved_ladder + occupied) * final_keep
    return jnp.transpose(full, (1, 2, 0))


class Layout:
    def __init__(self, rows, cols, row_tiles, integral_tiles, groups):
        self.rows, self.cols, self.groups = rows, cols, groups
        self.row_tiles, self.integral_tiles = row_tiles, integral_tiles
        self.integral_at = groups * row_tiles
        self.owner_at = self.integral_at + groups * integral_tiles
        self.count_at = self.owner_at + groups
        self.items_at = self.count_at + 2
        self.width = -(-(self.items_at + ROW_SLOTS) // 128) * 128

    def amp(self, info, row, tile, col, local):
        return info[row * self.cols + col, 0, local * self.row_tiles + tile]

    def integral(self, info, row, tile, col, local):
        return info[row * self.cols + col, 0, self.integral_at + local * self.integral_tiles + tile]

    def owner(self, info, row, col):
        return info[col, 0, self.owner_at + row]


def present(code):
    return jnp.minimum(code, 1)


def slot_rows(slot):
    return pl.ds(pl.multiple_of(slot * HALF, HALF), HALF)


def unfold(packed):
    return jnp.concatenate([packed[:, :TS], packed[:, TS:]], axis=0)


def fold(tile):
    return jnp.concatenate([tile[:HALF], tile[HALF:]], axis=1)


def iota(shape, axis):
    return lax.broadcasted_iota(jnp.int32, shape, axis)


def pack_kernel(
    lay, amp_bits, int_bits, extent, amp_vec, int_vec, owner_vec, amps, ints, packed, info_out, blocks, turn, items, limits, sems
):
    n_amp = jnp.int32(0)
    for local in range(lay.groups):
        for tile in range(lay.row_tiles):
            items[n_amp] = tile * 256 + local
            n_amp += amp_bits[local, tile]
    n_all = n_amp
    for local in range(lay.groups):
        for tile in range(lay.integral_tiles):
            items[n_all] = tile * 256 + local
            n_all += int_bits[local, tile]
    some_amp = jnp.minimum(n_amp, ROW_SLOTS)
    some = jnp.minimum(n_all, ROW_SLOTS)

    def fetch(source, slot):
        item = items[slot]
        rows = pl.ds(pl.multiple_of((item >> 8) * TS, TS), TS)
        lanes = pl.ds(pl.multiple_of(((item & 255) >> 1) * LANES, LANES), LANES)
        return pltpu.make_async_copy(source.at[rows, lanes], blocks.at[slot], sems.at[slot])

    def start_amp(slot, carry):
        fetch(amps, slot).start()
        limits[slot] = extent[items[slot] & 255]
        return carry

    def start_int(slot, carry):
        fetch(ints, slot).start()
        limits[slot] = TS
        return carry

    lax.fori_loop(0, some_amp, start_amp, 0)
    lax.fori_loop(some_amp, some, start_int, 0)
    pieces = [amp_vec[q : q + 1, :] for q in range(lay.groups)]
    pieces += [int_vec[q : q + 1, :] for q in range(lay.groups)]
    pieces += [owner_vec[...], jnp.zeros((1, lay.width - lay.count_at), jnp.int32)]
    entries = jnp.concatenate(pieces, axis=1).astype(jnp.float32)
    lane = iota((1, lay.width), 1)
    bits = jnp.where(lane < lay.owner_at, entries, 0.0)
    ahead = (iota((lay.width, lay.width), 0) <= iota((lay.width, lay.width), 1)).astype(jnp.float32)
    ranks = jnp.dot(
        jnp.broadcast_to(bits, (8, lay.width)), ahead, preferred_element_type=jnp.float32
    )[:1]
    row = jnp.where(lane < lay.owner_at, bits * ranks, entries).astype(jnp.int32)
    row = jnp.where(lane == lay.count_at, n_all, row)
    row = jnp.where(lane == lay.count_at + 1, n_amp, row)
    for slot in range(ROW_SLOTS):
        row = jnp.where(lane == lay.items_at + slot, items[slot], row)
    info_out[...] = jnp.broadcast_to(row[None], info_out.shape)

    def wait_amp(slot, carry):
        fetch(amps, slot).wait()
        return carry

    def wait_int(slot, carry):
        fetch(ints, slot).wait()
        return carry

    lax.fori_loop(0, some_amp, wait_amp, 0)
    lax.fori_loop(some_amp, some, wait_int, 0)
    position = iota((HALF, TS), 0)

    def place(index, carry):
        slots = [jnp.minimum(4 * index + j, some - 1) for j in range(4)]
        for j, slot in enumerate(slots):
            turn[j] = blocks[slot].T
        for j, slot in enumerate(slots):
            start = pl.multiple_of((items[slot] & 1) * TS, TS)
            upper = turn[j, pl.ds(start, HALF), :]
            lower = turn[j, pl.ds(start + HALF, HALF), :]
            upper = jnp.where(position < limits[slot], upper, 0.0)
            lower = jnp.where(position + HALF < limits[slot], lower, 0.0)
            packed[slot_rows(slot), :] = jnp.concatenate([upper, lower], axis=1)
        return carry

    lax.fori_loop(0, (some + 3) >> 2, place, 0)


def check_kernel(lay, info, result):
    codes = info[:, 0, :]
    here = jnp.minimum(codes, 1).astype(jnp.float32)
    lane = iota((1, lay.width), 1)
    contract = (((1,), (1,)), ((), ()))

    def field(start, length, block):
        shift = (lay.width - start) % lay.width
        moved = pltpu.roll(here, shift, 1) if shift else here
        return jnp.where(lane < length, moved, 0.0).reshape(lay.rows, lay.cols, lay.width)[block]

    shared = None
    for row in range(lay.rows):
        stack = jnp.concatenate(
            [field(q * lay.row_tiles, lay.row_tiles, row) for q in range(lay.groups)], axis=0
        )
        term = lax.dot_general(stack, stack, contract, preferred_element_type=jnp.float32)
        shared = term if shared is None else shared + term
    total = lay.groups * lay.cols
    tiles = lay.rows * lay.integral_tiles
    at, to = iota((total, tiles), 0), iota((total, tiles), 1)
    order = (at == (to % lay.groups) * lay.cols + to // lay.groups).astype(jnp.float32)
    shared = jnp.dot(shared, order, preferred_element_type=jnp.float32)
    at, to = iota((total, tiles), 0), iota((total, tiles), 1)
    own = to == (at % lay.cols) * lay.groups + at // lay.cols
    shared = jnp.where(own, 0.0, shared)
    counts = None
    for row in range(lay.rows):
        stack = jnp.concatenate(
            [
                field(lay.integral_at + q * lay.integral_tiles, lay.integral_tiles, row)
                for q in range(lay.groups)
            ],
            axis=0,
        )
        wide = stack[:, : lay.integral_tiles]
        mine = wide * shared[:, row * lay.integral_tiles : (row + 1) * lay.integral_tiles]
        at, to = iota((lay.integral_tiles, 128), 0), iota((lay.integral_tiles, 128), 1)
        group = (at // lay.groups == to).astype(jnp.float32)
        term = jnp.dot(mine, group, preferred_element_type=jnp.float32)
        counts = term if counts is None else jnp.maximum(counts, term)
    most = jnp.max(counts)
    used = jnp.max(jnp.where(lane == lay.count_at, codes, 0))
    level = jnp.where(most > COL_SLOTS[0], 1, 0)
    result[0] = jnp.where((most > COL_SLOTS[1]) | (used > ROW_SLOTS), 2, level)


def forward_kernel(lay, slots, info, *refs):
    packed, (out, pairs, lists, counts) = refs[: lay.rows], refs[lay.rows :]
    row, col = lax.axis_index("row"), lax.axis_index("col")
    base = col * lay.groups
    int_row, int_tile = base // lay.integral_tiles, base % lay.integral_tiles
    n_pairs = jnp.int32(0)
    for target in range(lay.cols):
        wanted = lay.owner(info, row, target)
        for local in range(lay.groups):
            pairs[n_pairs] = (target * 256 + local) * 256 + wanted
            hit = present(lay.integral(info, int_row, int_tile + local, target, wanted))
            n_pairs += jnp.where((target == col) & (wanted == local), 0, hit)
    for local in range(lay.groups):
        counts[local] = 0
    for k in range(lay.rows):
        device = (row ^ k) * lay.cols + col

        def sort(slot, carry, k=k, device=device):
            item = info[device, 0, lay.items_at + slot]
            local = item & 255
            count = counts[local]
            lists[local, count] = ((item >> 8) * 256 + slot) * 256 + k
            counts[local] = count + 1
            return carry

        lax.fori_loop(
            0, jnp.minimum(info[device, 0, lay.count_at + 1], ROW_SLOTS), sort, 0
        )

    def scan(index, carry):
        previous, slot = carry
        pair = pairs[index]
        wanted, local, target = pair & 255, (pair >> 8) & 255, pair >> 16

        def per_tile(index, slot):
            item = lists[local, index]
            which, source, tile = item & 255, (item >> 8) & 255, item >> 16
            hit = present(lay.amp(info, row ^ which, tile, target, wanted))

            @pl.when((hit > 0) & (slot < slots))
            def _():
                for k in range(lay.rows):

                    @pl.when(which == k)
                    def _():
                        out[target, slot_rows(slot), :] = packed[k][slot_rows(source), :]

            return slot + hit

        slot = jnp.where(target == previous, slot, 0)
        return target, lax.fori_loop(0, counts[local], per_tile, slot)

    lax.fori_loop(0, n_pairs, scan, (jnp.int32(-1), jnp.int32(0)))


def occupied_kernel(lay, info, extent, fock_scalar, fock, *refs):
    packed = refs[: lay.rows]
    out, todo, amp_id, int_id, next_slot, tiles, sums = refs[lay.rows :]
    row, col = lax.axis_index("row"), lax.axis_index("col")
    local = lay.owner(info, row, col)
    limit = extent[local]
    out[...] = jnp.zeros_like(out)
    for source in range(lay.cols):
        next_slot[source] = 0
    n_amp = jnp.int32(0)
    n_int = jnp.int32(0)
    for k in range(lay.rows):
        first = n_amp
        for tile in range(lay.row_tiles):
            code = lay.amp(info, row ^ k, tile, col, local)
            amp_id[n_amp] = ((row ^ k) * lay.row_tiles + tile) * 256 + code
            n_amp += present(code)

        def take_amp(index, carry, k=k):
            slot = jnp.minimum((amp_id[index] & 255) - 1, ROW_SLOTS - 1)
            tiles[slot_rows(index), :] = packed[k][slot_rows(slot), :]
            return carry

        lax.fori_loop(first, n_amp, take_amp, 0)
        for tile in range(lay.integral_tiles):
            code = lay.integral(info, row ^ k, tile, col, local)
            int_id[n_int] = (((row ^ k) * lay.integral_tiles + tile) * 256 + k) * 256 + code
            n_int += present(code)
    for beyond in range(4):
        amp_id[n_amp + beyond] = 0
        tiles[slot_rows(n_amp + beyond), :] = jnp.zeros((HALF, LANES), jnp.float32)

    blank = jnp.zeros((TS, TS), jnp.float32)
    both = jnp.concatenate(
        [
            jnp.concatenate([fock[...], blank], axis=1),
            jnp.concatenate([blank, fock[...]], axis=1),
        ],
        axis=0,
    )
    chunk = 4 * HALF

    def second(index, carry):
        rows = pl.ds(pl.multiple_of(index * chunk, chunk), chunk)
        sums[rows, :] = lax.dot_general(
            tiles[rows, :],
            both,
            (((1,), (1,)), ((), ())),
            precision=HIGHEST,
            preferred_element_type=jnp.float32,
        )
        return carry

    lax.fori_loop(0, (n_amp + 3) >> 2, second, 0)

    def int_slot(item):
        return jnp.minimum((item & 255) - 1, ROW_SLOTS - 1)

    def ladder(which, listed):
        item = int_id[which]
        middle = item >> 16
        source, middle_local = middle // lay.groups, middle % lay.groups
        own = (source == col) & (middle_local == local)
        own_row = middle // lay.integral_tiles

        for k in range(lay.rows):

            @pl.when(own & (row ^ k == own_row))
            def _():
                integral = unfold(packed[k][slot_rows(int_slot(item)), :])

                def diagonal(index, carry):
                    pair = [unfold(tiles[slot_rows(2 * index + j), :]) for j in range(2)]
                    product = jnp.dot(
                        integral,
                        jnp.concatenate(pair, axis=1),
                        precision=HIGHEST,
                        preferred_element_type=jnp.float32,
                    )
                    product = jnp.where(iota((TS, LANES), 0) < limit, product, 0.0)
                    sums[slot_rows(2 * index), :] += fold(product[:, :TS])
                    sums[slot_rows(2 * index + 1), :] += fold(product[:, TS:])
                    return carry

                lax.fori_loop(0, (n_amp + 1) >> 1, diagonal, 0)

        def arriving(index, listed):
            tile = amp_id[index] >> 8
            code = lay.amp(info, tile // lay.row_tiles, tile % lay.row_tiles, source, middle_local)
            slot = next_slot[source]
            todo[2 * listed] = (tile * 256 + source) * 256 + jnp.minimum(slot, 255)
            todo[2 * listed + 1] = ((item >> 8) & 255) * 256 + int_slot(item)
            hit = present(code)
            next_slot[source] = slot + hit
            return jnp.minimum(listed + hit, lay.cols * COL_SLOTS[1])

        return lax.fori_loop(0, jnp.where(own, 0, n_amp), arriving, listed)

    todo[2 * lay.cols * COL_SLOTS[1] + 2] = lax.fori_loop(0, n_int, ladder, jnp.int32(0))
    todo[2 * lay.cols * COL_SLOTS[1] + 3] = limit

    def write(index, carry):
        tile = amp_id[index] >> 8

        def first(step, values):
            values = list(values)
            for j in range(4):
                other = 4 * step + j
                scale = fock_scalar[tile, amp_id[other] >> 8]
                values[j & 1] = values[j & 1] + scale * tiles[slot_rows(other), :]
            return tuple(values)

        start = (sums[slot_rows(index), :], jnp.zeros((HALF, LANES), jnp.float32))
        value, other = lax.fori_loop(0, (n_amp + 3) >> 2, first, start)
        value = value + other
        turned = pltpu.roll(value, TS, 1)
        odd = tile & 1
        lanes = pl.ds(pl.multiple_of((tile >> 1) * LANES, LANES), LANES)
        side = iota((HALF, LANES), 1) // TS == odd
        is_odd = iota((HALF, LANES), 0) * 0 + odd == 1
        upper = jnp.where(is_odd, turned, value)
        lower = jnp.where(is_odd, value, turned)
        out[0, :HALF, lanes] = jnp.where(side, upper, out[0, :HALF, lanes])
        out[0, HALF:, lanes] = jnp.where(side, lower, out[0, HALF:, lanes])
        return carry

    lax.fori_loop(0, n_amp, write, 0)


def ladder_kernel(lay, todo, received, partial, *refs):
    packed, (out, integral) = refs[: lay.rows], refs[lay.rows :]
    out[...] = partial[...]
    limit = todo[2 * lay.cols * COL_SLOTS[1] + 3]

    def add(index, carry):
        item, where = todo[2 * index], todo[2 * index + 1]
        slot, source, tile = item & 255, (item >> 8) & 255, item >> 16
        for k in range(lay.rows):

            @pl.when(where >> 8 == k)
            def _():
                integral[...] = packed[k][slot_rows(where & 255), :]

        product = jnp.dot(
            unfold(integral[...]),
            unfold(received[source, slot_rows(slot), :]),
            precision=HIGHEST,
            preferred_element_type=jnp.float32,
        )
        product = jnp.where(iota((TS, TS), 0) < limit, product, 0.0)
        side = iota((TS, LANES), 1) // TS == tile & 1
        lanes = pl.ds(pl.multiple_of((tile >> 1) * LANES, LANES), LANES)
        out[0, :, lanes] += jnp.where(side, jnp.concatenate([product, product], axis=1), 0.0)
        return carry

    lax.fori_loop(0, todo[2 * lay.cols * COL_SLOTS[1] + 2], add, 0)


def local(
    amplitudes, pp_integrals, hole_fock, tile_pattern, integral_pattern, tile_extent, tile_owner
):
    rows, cols = lax.axis_size("row"), lax.axis_size("col")
    groups = tile_extent.shape[0]
    arguments = (
        amplitudes,
        pp_integrals,
        hole_fock,
        tile_pattern,
        integral_pattern,
        tile_extent,
        tile_owner,
    )
    row_tiles, integral_tiles = tile_pattern.shape[0], integral_pattern.shape[0]
    if groups != rows or integral_tiles % groups or rows & (rows - 1):
        return dense(*arguments)
    lay = Layout(rows, cols, row_tiles, integral_tiles, groups)
    devices = rows * cols

    def smem(shape):
        return pltpu.SMEM(shape, jnp.int32)

    in_smem = pl.BlockSpec(memory_space=pltpu.SMEM)
    in_vmem = pl.BlockSpec(memory_space=pltpu.VMEM)
    params = pltpu.CompilerParams(vmem_limit_bytes=32 * 2**20)
    packed_shape = (ROW_SLOTS * HALF, LANES)

    packed, mine = pl.pallas_call(
        lambda *refs: pack_kernel(lay, *refs),
        out_shape=(
            jax.ShapeDtypeStruct(packed_shape, jnp.float32),
            jax.ShapeDtypeStruct((devices, 1, lay.width), jnp.int32),
        ),
        in_specs=[in_smem] * 3 + [in_vmem] * 3 + [pl.BlockSpec(memory_space=pl.ANY)] * 2,
        out_specs=(in_vmem, in_vmem),
        scratch_shapes=[
            pltpu.VMEM((ROW_SLOTS, TS, LANES), jnp.float32),
            pltpu.VMEM((4, LANES, TS), jnp.float32),
            smem(((row_tiles + integral_tiles) * groups + ROW_SLOTS,)),
            smem((ROW_SLOTS,)),
            pltpu.SemaphoreType.DMA((ROW_SLOTS,)),
        ],
        compiler_params=params,
        name="pack_tiles",
    )(
        tile_pattern.T,
        integral_pattern.T,
        tile_extent,
        tile_pattern.T,
        integral_pattern.T,
        tile_owner,
        amplitudes,
        pp_integrals,
    )

    def swapped(values, k):
        return lax.ppermute(values, "row", [(i, i ^ k) for i in range(rows)])

    shares = {0: packed, 1: swapped(packed, 1)}
    shares.update({k: swapped(packed, k) for k in range(2, rows, 2)})
    info = lax.all_to_all(mine, ("row", "col"), split_axis=0, concat_axis=0, tiled=True)
    info, shares = lax.optimization_barrier((info, shares))
    shares.update({k ^ 1: swapped(shares[k], 1) for k in range(2, rows, 2)})
    shares = [shares[k] for k in range(rows)]

    level = pl.pallas_call(
        lambda *refs: check_kernel(lay, *refs),
        out_shape=jax.ShapeDtypeStruct((1,), jnp.int32),
        in_specs=[in_vmem],
        out_specs=in_smem,
        compiler_params=params,
        name="check_slots",
    )(info)

    def forward(slots, info, *shares):
        col_send = pl.pallas_call(
            lambda *refs: forward_kernel(lay, slots, *refs),
            out_shape=jax.ShapeDtypeStruct((cols, slots * HALF, LANES), jnp.float32),
            in_specs=[in_smem] + [in_vmem] * rows,
            out_specs=in_vmem,
            scratch_shapes=[
                smem((cols * groups + 1,)),
                smem((groups, rows * ROW_SLOTS)),
                smem((groups,)),
            ],
            compiler_params=params,
            name="forward_tiles",
        )(info, *shares)
        return lax.all_to_all(col_send, "col", split_axis=0, concat_axis=0, tiled=True)

    received = forward(COL_SLOTS[0], info, *shares)

    out_shape = (1, TS, rows * row_tiles * TS)
    all_tiles_rows = rows * (row_tiles + 1) * HALF
    partial, todo = pl.pallas_call(
        lambda *refs: occupied_kernel(lay, *refs),
        out_shape=(
            jax.ShapeDtypeStruct(out_shape, jnp.float32),
            jax.ShapeDtypeStruct((2 * cols * COL_SLOTS[1] + 4,), jnp.int32),
        ),
        in_specs=[in_smem] * 3 + [in_vmem] * (1 + rows),
        out_specs=(in_vmem, in_smem),
        scratch_shapes=[
            smem((rows * row_tiles + 4,)),
            smem((rows * integral_tiles + 1,)),
            smem((cols,)),
            pltpu.VMEM((all_tiles_rows, LANES), jnp.float32),
            pltpu.VMEM((all_tiles_rows, LANES), jnp.float32),
        ],
        compiler_params=params,
        name="occupied_terms",
    )(info, tile_extent, hole_fock, hole_fock, *shares)

    def finish(info, received, todo, partial, shares, arguments):
        return pl.pallas_call(
            lambda *refs: ladder_kernel(lay, *refs),
            out_shape=jax.ShapeDtypeStruct(out_shape, jnp.float32),
            in_specs=[in_smem] + [in_vmem] * (2 + rows),
            out_specs=in_vmem,
            scratch_shapes=[pltpu.VMEM((HALF, LANES), jnp.float32)],
            compiler_params=params,
            name="ladder_terms",
        )(todo, received, partial, *shares)

    def more_slots(info, received, todo, partial, shares, arguments):
        received = forward(COL_SLOTS[1], info, *shares)
        return finish(info, received, todo, partial, shares, arguments)

    def all_tiles(info, received, todo, partial, shares, arguments):
        return dense(*arguments)

    return lax.switch(
        level[0],
        (finish, more_slots, all_tiles),
        info,
        received,
        todo,
        partial,
        tuple(shares),
        arguments,
    )


def solution(mesh):
    placed = (
        P("row", "col"),
        P("row", "col"),
        P(),
        P("row", "col"),
        P("row", "col"),
        P("col"),
        P("col", None),
    )
    return jax.shard_map(
        local, mesh=mesh, in_specs=placed, out_specs=P(("row", "col"), None, None), check_vma=False
    )
```
